512 devices in a mesh: dp: 64 (over y, z), mp: 8 (over x, core).
Axes of the slice: x: 4, y: 8, z: 8, core: 2. Of those that a mesh axis runs over, the one named last changes fastest.
Arguments:
- tokens: bfloat16 [16384, 5376], P('dp', 'mp'), may hold values from -32 to 32
- factor_old: float32 [1344, 5376], P('dp', 'mp'), may hold values from -0.15 to 2.1
- basis: float32 [5376, 1344], P('mp'), may hold values from -0.15625 to 0.15625
Outputs:
- factor_new: float32 [1344, 5376], P('dp', 'mp')
- rotated: float32 [1344, 5376], P('dp', 'mp')
The draws below stay inside these ranges and needn't reach their ends.
All inputs are finite; a program needn't handle non-finite values.
Results may differ from the reference program's by a relative error of at most 0.0003.
Values may be sent and summed in bfloat16 or wider, within the bound.
A program may use at most 64 MiB of HBM per device.

```python
import jax
import jax.numpy as jnp
from jax import lax

D = 5376
TOKENS = 16384
BLK = 1344
NBLK = 4


def draw_tokens(key, part):
    key = jax.random.fold_in(key, 11)
    subkeys = jax.random.split(key, 5)
    noise_draw = jnp.clip(jax.random.normal(subkeys[0], (TOKENS, D), jnp.float32), -3.0, 3.0)
    placing = jnp.arange(TOKENS, dtype=jnp.float32) / TOKENS
    row_scale = jnp.exp(jax.random.uniform(subkeys[1], (TOKENS, 1), jnp.float32, jnp.log(0.5), jnp.log(1.5)))
    row_scale = row_scale * (0.6 + 1.2 * placing)[:, None]
    col_scale = jnp.exp(jax.random.uniform(subkeys[2], (1, D), jnp.float32, jnp.log(0.7), jnp.log(5.0)))
    loadings = jnp.clip(jax.random.normal(subkeys[3], (TOKENS, 4), jnp.float32), -3.0, 3.0) * 0.25
    patterns = jax.random.uniform(subkeys[4], (4, D), jnp.float32, -1.0, 1.0)
    combined = noise_draw
    for number in range(4):
        combined = combined + loadings[:, number:number + 1] * patterns[number:number + 1, :]
    values = combined * row_scale * col_scale
    return jnp.clip(values, -32.0, 32.0).astype(jnp.bfloat16)


def draw_factor_old(key, part):
    key = jax.random.fold_in(key, 23)
    subkeys = jax.random.split(key, 2)
    noise_draw = jnp.clip(jax.random.normal(subkeys[0], (BLK, NBLK, BLK), jnp.float32), -4.0, 4.0)
    levels = jnp.exp(jax.random.uniform(subkeys[1], (NBLK, BLK), jnp.float32, jnp.log(2.0), jnp.log(30.0)))
    mirrored = 0.5 * (noise_draw + jnp.transpose(noise_draw, (2, 1, 0)))
    row_level = jnp.transpose(levels)[:, :, None]
    col_level = levels[None, :, :]
    row_ids = jnp.arange(BLK, dtype=jnp.int32)[:, None, None]
    col_ids = jnp.arange(BLK, dtype=jnp.int32)[None, None, :]
    diagonal = jnp.where(row_ids == col_ids, 0.05 * col_level, 0.0)
    values = diagonal + 0.001 * mirrored * jnp.sqrt(row_level * col_level)
    return values.reshape(BLK, D).astype(jnp.float32)


def shard_levels(rng, extent, cuts, low, largest):
    def one(axis_at, blocks):
        heights = jax.random.uniform(jax.random.fold_in(jax.random.fold_in(rng, 6), axis_at), (blocks,), jnp.float32, low / len(cuts), largest / len(cuts))
        return jnp.repeat(jnp.exp(heights), extent[axis_at] // blocks).reshape((-1,) + (1,) * (len(extent) - axis_at - 1))

    gain = one(*cuts[0])
    for cut in cuts[1:]:
        gain = gain * one(*cut)
    return gain


def scatter_about(stream_key, shape, width, most, cuts=(), held_as=jnp.bfloat16):
    result = width * jax.random.normal(stream_key, shape, jnp.float32)
    if cuts:
        result = result * shard_levels(stream_key, shape, cuts, -0.22, 0.18)
    return jnp.clip(result, -most, most).astype(held_as)


def setup_inputs(seed: int = 0) -> dict:
    streams_of = jax.random.split(jax.random.key(seed), 4)
    tokens = draw_tokens(jax.random.fold_in(streams_of[3], 71), 0)
    factor_old = draw_factor_old(jax.random.fold_in(streams_of[3], 71), 0)
    basis = scatter_about(streams_of[2], (D, BLK), BLK ** -0.5, 0.15625, ((0, 8),), jnp.float32)
    return {"tokens": tokens, "factor_old": factor_old, "basis": basis}


decay_rate = 0.95


def reference(tokens, factor_old, basis):
    widened = tokens.astype(jnp.float32)
    gram_parts = []
    rotated_parts = []
    for number in range(D // BLK):
        columns = widened[:, number * BLK:(number + 1) * BLK]
        gram_block = jnp.dot(columns.T, columns, precision=lax.Precision.HIGHEST)
        gram_parts.append(gram_block)
    gram = jnp.concatenate(gram_parts, axis=1)
    factor_new = decay_rate * factor_old + ((1.0 - decay_rate) / TOKENS) * gram
    for number in range(D // BLK):
        left_part = factor_new[:, number * BLK:(number + 1) * BLK]
        right_part = basis[number * BLK:(number + 1) * BLK, :]
        rotated_parts.append(jnp.dot(left_part, right_part, precision=lax.Precision.HIGHEST))
    rotated = jnp.concatenate(rotated_parts, axis=1)
    return factor_new, rotated
```

```python
import jax
import jax.numpy as jnp
from jax import lax
from jax.experimental import pallas as pl
from jax.experimental.pallas import tpu as pltpu
from jax.sharding import PartitionSpec as P

decay_rate = 0.95

MESH = pl.DeviceIdType.MESH
SIDE = 8
ROWS = 21
CHUNK = SIDE * ROWS
PAD = 176
HALF = 672
PIECES = 3
WIDE = 256
WIDTHS = (256, 256, 160)
RIGHT, LEFT = 0, 1
FIRST = (((0, 256), (0, 128), None), (None, (128, 256), (0, 256)))
ORDER = ((2, 0, 1), (0, 2, 1))
OFFSETS = (4, 3, -3, 2, -2, 1, -1)


def encode(value):
    return ((value * jnp.abs(value)) * (value * value)).astype(jnp.bfloat16)


def decode(code):
    code = code.astype(jnp.float32)
    root = lax.rsqrt(lax.rsqrt(jnp.abs(code)))
    return jnp.where(code < 0.0, -root, root)


def kernel(
    scale_new, tok, old, bas, f_out, r_out,
    own_x, par_x, gram, sums, sent, got, flat, codes, far, fac,
    base, base_hi, base_lo, prod, prod_got,
    load_sem, par_sem, s_send, s_recv, t_send, t_recv, p_send, p_recv, ready,
):
    dp, mp = lax.axis_index("dp"), lax.axis_index("mp")
    y, z, core = dp // SIDE, dp % SIDE, mp % 2
    not_core = 1 - core
    here = not_core * y + core * z
    across = core * y + not_core * z

    def along(step):
        to_y = (y + not_core * step + SIDE) % SIDE
        to_z = (z + core * step + SIDE) % SIDE
        return {"dp": to_y * SIDE + to_z, "mp": mp}

    def cross(step):
        to_y = (y + core * step + SIDE) % SIDE
        to_z = (z + not_core * step + SIDE) % SIDE
        return {"dp": to_y * SIDE + to_z, "mp": mp}

    partner = {"dp": dp, "mp": mp + 1 - 2 * core}

    load_x = pltpu.make_async_copy(tok, own_x, load_sem.at[0])
    load_b = pltpu.make_async_copy(bas, base, load_sem.at[1])
    load_f = pltpu.make_async_copy(old, fac, load_sem.at[2])
    barrier = pltpu.get_barrier_semaphore()
    for device in (partner, along(1), along(-1), cross(1), cross(-1)):
        pl.semaphore_signal(barrier, inc=1, device_id=device, device_id_type=MESH)
    load_x.start()
    load_b.start()
    load_f.start()
    pl.semaphore_wait(barrier, 5)
    give_x = pltpu.make_async_remote_copy(
        src_ref=tok, dst_ref=par_x, send_sem=par_sem.at[0], recv_sem=par_sem.at[1],
        device_id=partner, device_id_type=MESH,
    )
    give_x.start()

    def announce(number):
        for device in (cross(1), cross(-1)):
            pl.semaphore_signal(
                ready.at[number], inc=1, device_id=device, device_id_type=MESH
            )

    announce(0)
    load_x.wait()
    give_x.wait()

    row = lax.broadcasted_iota(jnp.int32, (PAD, 1), 0)
    group = (row * 3121) >> 16
    col_id = lax.broadcasted_iota(jnp.int32, (PAD, HALF), 1)

    def products(slot, position):
        in_y = CHUNK * position + row
        in_z = ROWS * position + CHUNK * group + (row - ROWS * group)
        feature = not_core * in_y + core * in_z
        feature = jnp.where(row < CHUNK, feature, -2 * HALF)
        picked = jnp.zeros((PAD, own_x.shape[0]), jnp.float32)
        for block, first in ((own_x, HALF * core), (par_x, HALF * not_core)):
            pick = jnp.where(col_id == feature - first, 1.0, 0.0).astype(jnp.bfloat16)
            picked += lax.dot_general(
                pick, block[...], (((1,), (1,)), ((), ())),
                preferred_element_type=jnp.float32,
            )
        left = picked.astype(jnp.bfloat16)
        for piece, width in enumerate(WIDTHS):
            gram[slot, piece, :, 0:width] = jnp.dot(
                left, own_x[:, WIDE * piece:WIDE * piece + width],
                preferred_element_type=jnp.float32,
            )

    def slot_of(way, step):
        return 0 if step == 0 else 2 * step - 1 + way

    def hop(way, step, piece):
        lanes = FIRST[way][piece] if step == 0 else (0, WIDE)
        here_at = (way, step, piece, slice(None), slice(*lanes))
        return pltpu.make_async_remote_copy(
            src_ref=sent.at[here_at], dst_ref=got.at[here_at],
            send_sem=s_send.at[way, step, piece], recv_sem=s_recv.at[way, step, piece],
            device_id=along(1 if way == RIGHT else -1), device_id_type=MESH,
        )

    def put(way, step, piece):
        arrived = FIRST[way][piece] if step == 1 else (0, WIDTHS[piece])
        if step == 0:
            lo, hi = FIRST[way][piece]
            hi = min(hi, WIDTHS[piece])
            sent[way, step, piece, :, lo:hi] = encode(gram[0, piece, :, lo:hi])
        else:
            slot = slot_of(way, step)
            if arrived is None:
                arrived = (0, 0)
            lo, hi = arrived
            hi = min(hi, WIDTHS[piece])
            if hi > lo:
                hop(way, step - 1, piece).wait_recv()
                total = gram[slot, piece, :, lo:hi] + decode(got[way, step - 1, piece, :, lo:hi])
                sent[way, step, piece, :, lo:hi] = encode(total)
            for a, b in ((0, lo), (hi, WIDTHS[piece])):
                if b > a:
                    sent[way, step, piece, :, a:b] = encode(gram[slot, piece, :, a:b])
        hop(way, step, piece).start()

    products(0, (here + 4) % SIDE)
    put(RIGHT, 0, 0)
    put(LEFT, 0, 2)
    put(RIGHT, 0, 1)
    put(LEFT, 0, 1)
    products(1, (here + 3) % SIDE)
    put(RIGHT, 1, ORDER[RIGHT][0])
    products(2, (here + 5) % SIDE)
    put(LEFT, 1, ORDER[LEFT][0])
    for place in (1, 2):
        put(RIGHT, 1, ORDER[RIGHT][place])
        put(LEFT, 1, ORDER[LEFT][place])
    pl.semaphore_wait(ready.at[0], 2)
    announce(1)
    products(3, (here + 2) % SIDE)
    products(4, (here + 6) % SIDE)
    for place in range(PIECES):
        put(RIGHT, 2, ORDER[RIGHT][place])
        put(LEFT, 2, ORDER[LEFT][place])
    pl.semaphore_wait(ready.at[1], 2)
    announce(2)
    products(5, (here + 1) % SIDE)
    products(6, (here + 7) % SIDE)
    for place in range(PIECES):
        put(RIGHT, 3, ORDER[RIGHT][place])
        put(LEFT, 3, ORDER[LEFT][place])
    products(7, here)
    load_b.wait()

    @pl.loop(0, HALF // 96)
    def _(part):
        at = pl.ds(pl.multiple_of(part * 96, 96), 96)
        for half in range(2):
            value = base[at, HALF * half:HALF * (half + 1)]
            high = value.astype(jnp.bfloat16)
            base_hi[half, at, :] = high
            base_lo[half, at, :] = (value - high.astype(jnp.float32)).astype(jnp.bfloat16)

    pl.semaphore_wait(ready.at[2], 2)

    def over(number, piece):
        to = (across + OFFSETS[number] + SIDE) % SIDE
        return pltpu.make_async_remote_copy(
            src_ref=codes.at[to, pl.ds(48 * piece, 48)],
            dst_ref=far.at[number, pl.ds(48 * piece, 48)],
            send_sem=t_send.at[number, piece], recv_sem=t_recv.at[number, piece],
            device_id=cross(OFFSETS[number]), device_id_type=MESH,
        )

    for piece in (0, 2, 1):
        width = WIDTHS[piece]
        hop(RIGHT, 3, piece).wait_recv()
        hop(LEFT, 3, piece).wait_recv()
        sums[piece, :, 0:width] = (
            gram[7, piece, :, 0:width]
            + decode(got[RIGHT, 3, piece, :, 0:width])
            + decode(got[LEFT, 3, piece, :, 0:width])
        )
        for to in range(SIDE):
            both = jnp.concatenate(
                [sums[piece, ROWS * to:ROWS * to + 24, 128 * t:128 * t + 128] for t in range(2)], 0
            )
            flat[to, 48 * piece:48 * piece + 48, :] = both
            codes[to, 48 * piece:48 * piece + 48, :] = encode(both)
        for number in range(len(OFFSETS)):
            over(number, piece).start()

    load_f.wait()
    for piece in (0, 2, 1):
        total = flat[across, 48 * piece:48 * piece + 48, :]
        for number in range(len(OFFSETS)):
            over(number, piece).wait_recv()
            total += decode(far[number, 48 * piece:48 * piece + 48, :])
        for t in range(2):
            lo = WIDE * piece + 128 * t
            hi = min(lo + 128, HALF)
            part = total[24 * t:24 * t + ROWS, 0:hi - lo]
            f_out[:, lo:hi] = decay_rate * fac[:, lo:hi] + scale_new * part

    value = f_out[...]
    value = jnp.concatenate([value, jnp.zeros((32 - ROWS, HALF), jnp.float32)], 0)
    high = value.astype(jnp.bfloat16)
    low = (value - high.astype(jnp.float32)).astype(jnp.bfloat16)
    both = jnp.concatenate([high, low], 0)

    def turned(half):
        main = jnp.dot(both, base_hi[half], preferred_element_type=jnp.float32)
        rest = jnp.dot(high, base_lo[half], preferred_element_type=jnp.float32)
        return main[0:24] + (main[32:56] + rest[0:24])

    prod[...] = turned(not_core)
    give_r = pltpu.make_async_remote_copy(
        src_ref=prod, dst_ref=prod_got, send_sem=p_send, recv_sem=p_recv,
        device_id=partner, device_id_type=MESH,
    )
    give_r.start()
    mine = turned(core)
    give_r.wait()
    r_out[...] = mine[0:ROWS] + prod_got[0:ROWS, :]

    for way in range(2):
        for step in range(4):
            for piece in range(PIECES):
                if step > 0 or FIRST[way][piece] is not None:
                    hop(way, step, piece).wait_send()
    for number in range(len(OFFSETS)):
        for piece in range(PIECES):
            over(number, piece).wait_send()


def shards(tokens, factor_old, basis):
    tok_rows, features = tokens.shape
    scale_new = (1.0 - decay_rate) / (tok_rows * lax.axis_size("dp"))
    f32, bf16 = jnp.float32, jnp.bfloat16
    body = lambda *refs: kernel(scale_new, *refs)
    dma = pltpu.SemaphoreType.DMA
    return pl.pallas_call(
        body,
        name="gram_rotate",
        out_shape=(
            jax.ShapeDtypeStruct((ROWS, HALF), f32),
            jax.ShapeDtypeStruct((ROWS, HALF), f32),
        ),
        in_specs=[pl.BlockSpec(memory_space=pl.ANY)] * 3,
        out_specs=[pl.BlockSpec(memory_space=pltpu.VMEM)] * 2,
        scratch_shapes=[
            pltpu.VMEM((tok_rows, HALF), bf16),
            pltpu.VMEM((tok_rows, HALF), bf16),
            pltpu.VMEM((SIDE, PIECES, PAD, WIDE), f32),
            pltpu.VMEM((PIECES, PAD, WIDE), f32),
            pltpu.VMEM((2, 4, PIECES, PAD, WIDE), bf16),
            pltpu.VMEM((2, 4, PIECES, PAD, WIDE), bf16),
            pltpu.VMEM((SIDE, 48 * PIECES, 128), f32),
            pltpu.VMEM((SIDE, 48 * PIECES, 128), bf16),
            pltpu.VMEM((SIDE - 1, 48 * PIECES, 128), bf16),
            pltpu.VMEM((ROWS, HALF), f32),
            pltpu.VMEM((HALF, 2 * HALF), f32),
            pltpu.VMEM((2, HALF, HALF), bf16),
            pltpu.VMEM((2, HALF, HALF), bf16),
            pltpu.VMEM((24, HALF), f32),
            pltpu.VMEM((24, HALF), f32),
            dma((3,)),
            dma((2,)),
            dma((2, 4, PIECES)),
            dma((2, 4, PIECES)),
            dma((SIDE - 1, PIECES)),
            dma((SIDE - 1, PIECES)),
            dma,
            dma,
            pltpu.SemaphoreType.REGULAR((3,)),
        ],
        compiler_params=pltpu.CompilerParams(
            collective_id=0, has_side_effects=True, vmem_limit_bytes=48 * 2**20
        ),
    )(tokens, factor_old, basis)


def solution(mesh):
    return jax.shard_map(
        shards,
        mesh=mesh,
        in_specs=(P("dp", "mp"), P("dp", "mp"), P("mp", None)),
        out_specs=(P("dp", "mp"), P("dp", "mp")),
        check_vma=False,
    )
```

```python
import jax
import jax.numpy as jnp
from jax import lax
from jax.experimental import pallas as pl
from jax.experimental.pallas import tpu as pltpu
from jax.sharding import PartitionSpec as P

decay_rate = 0.95

MESH = pl.DeviceIdType.MESH
SIDE = 8
ROWS = 21
CHUNK = SIDE * ROWS
PAD = 176
HALF = 672
FULL = 5
REST = HALF - 128 * FULL
TAIL = FULL * PAD
LONG = TAIL + 48
PIECES = ((0, 352), (352, 704), (704, LONG))
FIRST = ((0, LONG // 2), (LONG // 2, LONG))
RIGHT, LEFT = 0, 1
ORDER = ((2, 0, 1), (0, 2, 1))
LAST = (0, 2, 1)
OFFSETS = (4, 3, -3, 2, -2, 1, -1)


def encode(value):
    return ((value * jnp.abs(value)) * (value * value)).astype(jnp.bfloat16)


def decode(code):
    code = code.astype(jnp.float32)
    root = lax.rsqrt(lax.rsqrt(jnp.abs(code)))
    return jnp.where(code < 0.0, -root, root)


def overlap(one, other):
    lo, hi = max(one[0], other[0]), min(one[1], other[1])
    return (lo, hi) if lo < hi else None


def turn_pieces(both, base_hi, base_lo, half, piece):
    lo, hi = 256 * piece, min(256 * piece + 256, HALF)
    out = jnp.dot(both, base_hi[half, lo:hi, :], preferred_element_type=jnp.float32)
    return out + jnp.dot(both, base_lo[half, lo:hi, :], preferred_element_type=jnp.float32)


def kernel(
    scale_new, tok, old, bas, f_out, r_out,
    own_x, par_x, wide_x, left_x, gram, sums, rest, sent, got, flat, codes, far, fac,
    base, base_hi, base_lo, prod, prod_got,
    load_sem, par_sem, s_send, s_recv, t_send, t_recv, p_send, p_recv, ready,
):
    dp, mp = lax.axis_index("dp"), lax.axis_index("mp")
    y, z, core = dp // SIDE, dp % SIDE, mp % 2
    not_core = 1 - core
    here = not_core * y + core * z
    across = core * y + not_core * z

    def along(step):
        to_y = (y + not_core * step + SIDE) % SIDE
        to_z = (z + core * step + SIDE) % SIDE
        return {"dp": to_y * SIDE + to_z, "mp": mp}

    def cross(step):
        to_y = (y + core * step + SIDE) % SIDE
        to_z = (z + not_core * step + SIDE) % SIDE
        return {"dp": to_y * SIDE + to_z, "mp": mp}

    partner = {"dp": dp, "mp": mp + 1 - 2 * core}

    load_x = pltpu.make_async_copy(tok, own_x, load_sem.at[0])
    load_b = pltpu.make_async_copy(bas, base, load_sem.at[1])
    load_f = pltpu.make_async_copy(old, fac, load_sem.at[2])
    barrier = pltpu.get_barrier_semaphore()
    for device in (partner, along(1), along(-1), cross(1), cross(-1)):
        pl.semaphore_signal(barrier, inc=1, device_id=device, device_id_type=MESH)
    load_x.start()
    wide_x[2 * HALF:2 * HALF + 8, :] = jnp.zeros((8, wide_x.shape[1]), jnp.float32)
    left_x[CHUNK:192, :] = jnp.zeros((192 - CHUNK, wide_x.shape[1]), jnp.float32)
    pl.semaphore_wait(barrier, 5)
    give_x = pltpu.make_async_remote_copy(
        src_ref=tok, dst_ref=par_x, send_sem=par_sem.at[0], recv_sem=par_sem.at[1],
        device_id=partner, device_id_type=MESH,
    )
    give_x.start()
    load_b.start()
    load_f.start()

    def announce(number):
        for device in (cross(1), cross(-1)):
            pl.semaphore_signal(
                ready.at[number], inc=1, device_id=device, device_id_type=MESH
            )

    announce(0)
    load_x.wait()
    wide_x[pl.ds(pl.multiple_of(HALF * core, 8), HALF), :] = own_x[...].astype(jnp.float32)
    give_x.wait()
    wide_x[pl.ds(pl.multiple_of(HALF * not_core, 8), HALF), :] = par_x[...].astype(jnp.float32)

    def products(slot, position):
        for group in range(SIDE):
            in_y = CHUNK * position + ROWS * group
            in_z = ROWS * position + CHUNK * group
            start = not_core * in_y + core * in_z
            block = wide_x[pl.ds(pl.multiple_of(start // 8 * 8, 8), 32), :]
            block = pltpu.roll(block, (32 - start % 8) % 32, 0)
            left_x[ROWS * group:ROWS * group + 24, :] = block[0:24]
        left = left_x[...].astype(jnp.bfloat16)
        main = lax.dot_general(
            left[0:PAD], own_x[0:128 * FULL, :], (((1,), (1,)), ((), ())),
            preferred_element_type=jnp.float32,
        )
        for tile in range(FULL):
            gram[slot, PAD * tile:PAD * (tile + 1), :] = main[:, 128 * tile:128 * (tile + 1)]
        thin = lax.dot_general(
            left, own_x[128 * FULL:HALF, :], (((1,), (1,)), ((), ())),
            preferred_element_type=jnp.float32,
        )
        gram[slot, TAIL:LONG, :] = jnp.concatenate(
            [thin[48 * k:48 * (k + 1)] for k in range(4)], 1
        )

    def slot_of(way, step):
        return 0 if step == 0 else 2 * step - 1 + way

    def rows_of(way, step, piece):
        return overlap(FIRST[way], PIECES[piece]) if step == 0 else PIECES[piece]

    def hop(way, step, piece):
        lo, hi = rows_of(way, step, piece)
        return pltpu.make_async_remote_copy(
            src_ref=sent.at[way, step, pl.ds(lo, hi - lo)],
            dst_ref=got.at[way, step, pl.ds(lo, hi - lo)],
            send_sem=s_send.at[way, step, piece], recv_sem=s_recv.at[way, step, piece],
            device_id=along(1 if way == RIGHT else -1), device_id_type=MESH,
        )

    def put(way, step, piece):
        slot = slot_of(way, step)
        lo, hi = rows_of(way, step, piece)
        arrived = rows_of(way, step - 1, piece) if step else None
        if arrived is None:
            sent[way, step, lo:hi, :] = encode(gram[slot, lo:hi, :])
        else:
            a, b = arrived
            for c, d in ((lo, a), (b, hi)):
                if c < d:
                    sent[way, step, c:d, :] = encode(gram[slot, c:d, :])
            hop(way, step - 1, piece).wait_recv()
            sent[way, step, a:b, :] = encode(
                gram[slot, a:b, :] + decode(got[way, step - 1, a:b, :])
            )
        hop(way, step, piece).start()

    def split_base(first, last):
        @pl.loop(first, last)
        def _(part):
            at = pl.ds(pl.multiple_of(part * 96, 96), 96)
            for half in range(2):
                value = base[at, HALF * half:HALF * (half + 1)]
                high = value.astype(jnp.bfloat16)
                base_hi[half, at, :] = high
                base_lo[half, at, :] = (value - high.astype(jnp.float32)).astype(jnp.bfloat16)

    products(0, (here + 4) % SIDE)
    put(RIGHT, 0, 0)
    put(LEFT, 0, 2)
    put(RIGHT, 0, 1)
    put(LEFT, 0, 1)
    products(1, (here + 3) % SIDE)
    put(RIGHT, 1, ORDER[RIGHT][0])
    products(2, (here + 5) % SIDE)
    put(LEFT, 1, ORDER[LEFT][0])
    products(3, (here + 2) % SIDE)
    products(4, (here + 6) % SIDE)
    for place in (1, 2):
        put(RIGHT, 1, ORDER[RIGHT][place])
        put(LEFT, 1, ORDER[LEFT][place])
    pl.semaphore_wait(ready.at[0], 2)
    announce(1)
    products(5, (here + 1) % SIDE)
    products(6, (here + 7) % SIDE)
    for place in range(3):
        put(RIGHT, 2, ORDER[RIGHT][place])
        put(LEFT, 2, ORDER[LEFT][place])
    pl.semaphore_wait(ready.at[1], 2)
    announce(2)
    products(7, here)
    load_b.wait()
    split_base(0, 4)
    for place in range(3):
        put(RIGHT, 3, ORDER[RIGHT][place])
        put(LEFT, 3, ORDER[LEFT][place])
    split_base(4, 7)
    pl.semaphore_wait(ready.at[2], 2)

    def over(number, piece):
        to = (across + OFFSETS[number] + SIDE) % SIDE
        return pltpu.make_async_remote_copy(
            src_ref=codes.at[to, pl.ds(48 * piece, 48)],
            dst_ref=far.at[number, pl.ds(48 * piece, 48)],
            send_sem=t_send.at[number, piece], recv_sem=t_recv.at[number, piece],
            device_id=cross(OFFSETS[number]), device_id_type=MESH,
        )

    for piece in LAST:
        lo, hi = PIECES[piece]
        hop(RIGHT, 3, piece).wait_recv()
        hop(LEFT, 3, piece).wait_recv()
        sums[lo:hi, :] = (
            gram[7, lo:hi, :] + decode(got[RIGHT, 3, lo:hi, :]) + decode(got[LEFT, 3, lo:hi, :])
        )
        if piece == 2:
            for k in range(4):
                rest[48 * k:48 * (k + 1), 0:REST] = sums[TAIL:LONG, REST * k:REST * (k + 1)]
        for to in range(SIDE):
            parts = []
            for tile in (2 * piece, 2 * piece + 1):
                if tile < FULL:
                    at = PAD * tile + ROWS * to
                    parts.append(sums[at:at + 24, :])
                else:
                    parts.append(rest[ROWS * to:ROWS * to + 24, :])
            both = jnp.concatenate(parts, 0)
            flat[to, 48 * piece:48 * piece + 48, :] = both
            codes[to, 48 * piece:48 * piece + 48, :] = encode(both)
        for number in range(len(OFFSETS)):
            over(number, piece).start()

    load_f.wait()
    fac_rows = []
    theirs = jnp.zeros((48, HALF), jnp.float32)
    mine = jnp.zeros((48, HALF), jnp.float32)
    for piece in LAST:
        total = flat[across, 48 * piece:48 * piece + 48, :]
        for number in range(len(OFFSETS)):
            over(number, piece).wait_recv()
            total += decode(far[number, 48 * piece:48 * piece + 48, :])
        lo, hi = 256 * piece, min(256 * piece + 256, HALF)
        gram_part = jnp.concatenate([total[0:24], total[24:48]], 1)[0:ROWS, 0:hi - lo]
        new = decay_rate * fac[:, lo:hi] + scale_new * gram_part
        f_out[:, lo:hi] = new
        new = jnp.concatenate([new, jnp.zeros((24 - ROWS, hi - lo), jnp.float32)], 0)
        high = new.astype(jnp.bfloat16).astype(jnp.float32)
        both = jnp.concatenate([high, new - high], 0).astype(jnp.bfloat16)
        theirs += turn_pieces(both, base_hi, base_lo, not_core, piece)
        if piece != LAST[-1]:
            mine += turn_pieces(both, base_hi, base_lo, core, piece)

    prod[...] = theirs[0:24] + theirs[24:48]
    give_r = pltpu.make_async_remote_copy(
        src_ref=prod, dst_ref=prod_got, send_sem=p_send, recv_sem=p_recv,
        device_id=partner, device_id_type=MESH,
    )
    give_r.start()
    mine += turn_pieces(both, base_hi, base_lo, core, LAST[-1])
    for way in range(2):
        for step in range(4):
            for piece in range(3):
                if rows_of(way, step, piece) is not None:
                    hop(way, step, piece).wait_send()
    for number in range(len(OFFSETS)):
        for piece in range(3):
            over(number, piece).wait_send()
    give_r.wait()
    r_out[...] = mine[0:ROWS] + mine[24:24 + ROWS] + prod_got[0:ROWS, :]


def shards(tokens, factor_old, basis):
    tok_rows, features = tokens.shape
    scale_new = (1.0 - decay_rate) / (tok_rows * lax.axis_size("dp"))
    f32, bf16 = jnp.float32, jnp.bfloat16
    body = lambda *refs: kernel(scale_new, *refs)
    dma = pltpu.SemaphoreType.DMA
    return pl.pallas_call(
        body,
        name="gram_rotate",
        out_shape=(
            jax.ShapeDtypeStruct((ROWS, HALF), f32),
            jax.ShapeDtypeStruct((ROWS, HALF), f32),
        ),
        in_specs=[pl.BlockSpec(memory_space=pl.ANY)] * 3,
        out_specs=[pl.BlockSpec(memory_space=pltpu.VMEM)] * 2,
        scratch_shapes=[
            pltpu.VMEM((HALF, tok_rows), bf16),
            pltpu.VMEM((HALF, tok_rows), bf16),
            pltpu.VMEM((2 * HALF + 8, tok_rows), f32),
            pltpu.VMEM((192, tok_rows), f32),
            pltpu.VMEM((SIDE, LONG, 128), f32),
            pltpu.VMEM((LONG, 128), f32),
            pltpu.VMEM((192, 128), f32),
            pltpu.VMEM((2, 4, LONG, 128), bf16),
            pltpu.VMEM((2, 4, LONG, 128), bf16),
            pltpu.VMEM((SIDE, 144, 128), f32),
            pltpu.VMEM((SIDE, 144, 128), bf16),
            pltpu.VMEM((SIDE - 1, 144, 128), bf16),
            pltpu.VMEM((ROWS, HALF), f32),
            pltpu.VMEM((HALF, 2 * HALF), f32),
            pltpu.VMEM((2, HALF, HALF), bf16),
            pltpu.VMEM((2, HALF, HALF), bf16),
            pltpu.VMEM((24, HALF), f32),
            pltpu.VMEM((24, HALF), f32),
            dma((3,)),
            dma((2,)),
            dma((2, 4, 3)),
            dma((2, 4, 3)),
            dma((SIDE - 1, 3)),
            dma((SIDE - 1, 3)),
            dma,
            dma,
            pltpu.SemaphoreType.REGULAR((3,)),
        ],
        compiler_params=pltpu.CompilerParams(
            collective_id=0, has_side_effects=True, vmem_limit_bytes=55040 * 1024
        ),
    )(tokens.T, factor_old, basis)


def solution(mesh):
    return jax.shard_map(
        shards,
        mesh=mesh,
        in_specs=(P("dp", "mp"), P("dp", "mp"), P("mp", None)),
        out_specs=(P("dp", "mp"), P("dp", "mp")),
        check_vma=False,
    )
```

```python
import jax
import jax.numpy as jnp
from jax import lax
from jax.experimental import pallas as pl
from jax.experimental.pallas import tpu as pltpu
from jax.sharding import PartitionSpec as P

decay_rate = 0.95

MESH = pl.DeviceIdType.MESH
SIDE = 8
ROWS = 21
CHUNK = SIDE * ROWS
PAD = 176
HALF = 672
FULL = 5
REST = HALF - 128 * FULL
LONG = FULL * PAD + 48
TILES = (0, PAD, 2 * PAD, 3 * PAD + 48, 4 * PAD + 48)
TAIL = 3 * PAD
PIECES = ((0, PAD), (PAD, 2 * PAD), (2 * PAD, TAIL + 48), (TILES[3], TILES[4]), (TILES[4], LONG))
GROUPS = ((0, 1), (3, 4), (2,))
COLUMNS = ((0, 1), (3, 4), (2, 5))
FIRST = ((0, LONG // 2), (LONG // 2, LONG))
RIGHT, LEFT = 0, 1
ORDER = ((3, 4, 0, 1, 2), (1, 0, 4, 3, 2))
OFFSETS = (4, 3, -3, 2, -2, 1, -1)


def encode(value):
    return ((value * jnp.abs(value)) * (value * value)).astype(jnp.bfloat16)


def decode(code):
    code = code.astype(jnp.float32)
    root = lax.rsqrt(lax.rsqrt(jnp.abs(code)))
    return jnp.where(code < 0.0, -root, root)


def overlap(one, other):
    lo, hi = max(one[0], other[0]), min(one[1], other[1])
    return (lo, hi) if lo < hi else None


def spans(group):
    return [(128 * tile, min(128 * tile + 128, HALF)) for tile in COLUMNS[group]]


def turned(both, base_hi, base_lo, half, group):
    out = jnp.zeros((48, HALF), jnp.float32)
    for part, (lo, hi) in zip(both, spans(group)):
        out += jnp.dot(part, base_hi[half, lo:hi, :], preferred_element_type=jnp.float32)
        out += jnp.dot(part, base_lo[half, lo:hi, :], preferred_element_type=jnp.float32)
    return out


def kernel(
    scale_new, tok, old, bas, f_out, r_out,
    own_x, par_x, wide_x, left_x, gram, sums, rest, sent, got, flat, codes, far, fac,
    base, base_hi, base_lo, prod, prod_got,
    load_sem, par_sem, s_send, s_recv, t_send, t_recv, p_send, p_recv, ready,
):
    dp, mp = lax.axis_index("dp"), lax.axis_index("mp")
    y, z, core = dp // SIDE, dp % SIDE, mp % 2
    not_core = 1 - core
    here = not_core * y + core * z
    across = core * y + not_core * z

    def along(step):
        to_y = (y + not_core * step + SIDE) % SIDE
        to_z = (z + core * step + SIDE) % SIDE
        return {"dp": to_y * SIDE + to_z, "mp": mp}

    def cross(step):
        to_y = (y + core * step + SIDE) % SIDE
        to_z = (z + not_core * step + SIDE) % SIDE
        return {"dp": to_y * SIDE + to_z, "mp": mp}

    partner = {"dp": dp, "mp": mp + 1 - 2 * core}

    load_x = pltpu.make_async_copy(tok, own_x, load_sem.at[0])
    load_b = pltpu.make_async_copy(bas, base, load_sem.at[1])
    load_f = pltpu.make_async_copy(old, fac, load_sem.at[2])
    barrier = pltpu.get_barrier_semaphore()
    for device in (partner, along(1), along(-1), cross(1), cross(-1)):
        pl.semaphore_signal(barrier, inc=1, device_id=device, device_id_type=MESH)
    load_x.start()
    wide_x[2 * HALF:2 * HALF + 8, :] = jnp.zeros((8, wide_x.shape[1]), jnp.float32)
    left_x[CHUNK:192, :] = jnp.zeros((192 - CHUNK, wide_x.shape[1]), jnp.float32)
    pl.semaphore_wait(barrier, 5)
    give_x = pltpu.make_async_remote_copy(
        src_ref=tok, dst_ref=par_x, send_sem=par_sem.at[0], recv_sem=par_sem.at[1],
        device_id=partner, device_id_type=MESH,
    )
    give_x.start()
    load_b.start()
    load_f.start()

    def announce(number):
        for device in (cross(1), cross(-1)):
            pl.semaphore_signal(
                ready.at[number], inc=1, device_id=device, device_id_type=MESH
            )

    announce(0)
    load_x.wait()
    wide_x[pl.ds(pl.multiple_of(HALF * core, 8), HALF), :] = own_x[...].astype(jnp.float32)
    give_x.wait()
    wide_x[pl.ds(pl.multiple_of(HALF * not_core, 8), HALF), :] = par_x[...].astype(jnp.float32)

    def products(slot, position):
        for group in range(SIDE):
            in_y = CHUNK * position + ROWS * group
            in_z = ROWS * position + CHUNK * group
            start = not_core * in_y + core * in_z
            block = wide_x[pl.ds(pl.multiple_of(start // 8 * 8, 8), 32), :]
            block = pltpu.roll(block, (32 - start % 8) % 32, 0)
            left_x[ROWS * group:ROWS * group + 24, :] = block[0:24]
        left = left_x[...].astype(jnp.bfloat16)
        main = lax.dot_general(
            left[0:PAD], own_x[0:128 * FULL, :], (((1,), (1,)), ((), ())),
            preferred_element_type=jnp.float32,
        )
        for tile in range(FULL):
            gram[slot, TILES[tile]:TILES[tile] + PAD, :] = main[:, 128 * tile:128 * (tile + 1)]
        thin = lax.dot_general(
            left, own_x[128 * FULL:HALF, :], (((1,), (1,)), ((), ())),
            preferred_element_type=jnp.float32,
        )
        gram[slot, TAIL:TAIL + 48, :] = jnp.concatenate(
            [thin[48 * k:48 * (k + 1)] for k in range(4)], 1
        )

    def slot_of(way, step):
        return 0 if step == 0 else 2 * step - 1 + way

    def rows_of(way, step, piece):
        return overlap(FIRST[way], PIECES[piece]) if step == 0 else PIECES[piece]

    def hop(way, step, piece):
        lo, hi = rows_of(way, step, piece)
        return pltpu.make_async_remote_copy(
            src_ref=sent.at[way, step, pl.ds(lo, hi - lo)],
            dst_ref=got.at[way, step, pl.ds(lo, hi - lo)],
            send_sem=s_send.at[way, step, piece], recv_sem=s_recv.at[way, step, piece],
            device_id=along(1 if way == RIGHT else -1), device_id_type=MESH,
        )

    def put(way, step, piece):
        slot = slot_of(way, step)
        lo, hi = rows_of(way, step, piece)
        arrived = rows_of(way, step - 1, piece) if step else None
        if arrived is None:
            sent[way, step, lo:hi, :] = encode(gram[slot, lo:hi, :])
        else:
            a, b = arrived
            for c, d in ((lo, a), (b, hi)):
                if c < d:
                    sent[way, step, c:d, :] = encode(gram[slot, c:d, :])
            hop(way, step - 1, piece).wait_recv()
            sent[way, step, a:b, :] = encode(
                gram[slot, a:b, :] + decode(got[way, step - 1, a:b, :])
            )
        hop(way, step, piece).start()

    def split_base(first, last):
        @pl.loop(first, last)
        def _(part):
            at = pl.ds(pl.multiple_of(part * 96, 96), 96)
            for half in range(2):
                value = base[at, HALF * half:HALF * (half + 1)]
                high = value.astype(jnp.bfloat16)
                base_hi[half, at, :] = high
                base_lo[half, at, :] = (value - high.astype(jnp.float32)).astype(jnp.bfloat16)

    def both_ways(step, places):
        for place in places:
            put(RIGHT, step, ORDER[RIGHT][place])
            put(LEFT, step, ORDER[LEFT][place])

    products(0, (here + 4) % SIDE)
    for place in range(3):
        put(RIGHT, 0, (0, 1, 2)[place])
        put(LEFT, 0, (4, 3, 2)[place])
    products(1, (here + 3) % SIDE)
    products(2, (here + 5) % SIDE)
    both_ways(1, (0, 1))
    products(3, (here + 2) % SIDE)
    products(4, (here + 6) % SIDE)
    both_ways(1, (2, 3, 4))
    pl.semaphore_wait(ready.at[0], 2)
    announce(1)
    products(5, (here + 1) % SIDE)
    products(6, (here + 7) % SIDE)
    both_ways(2, range(5))
    pl.semaphore_wait(ready.at[1], 2)
    announce(2)
    products(7, here)
    load_b.wait()
    split_base(0, 4)
    both_ways(3, range(5))
    split_base(4, 7)
    pl.semaphore_wait(ready.at[2], 2)

    def over(number, group):
        to = core * ((across + OFFSETS[number] + SIDE) % SIDE) + not_core * (
            number + jnp.where(across <= number, 1, 0)
        )
        away = (to - across + SIDE) % SIDE
        at = pl.ds(48 * group, 48)
        return pltpu.make_async_remote_copy(
            src_ref=codes.at[to, at], dst_ref=far.at[away - 1, at],
            send_sem=t_send.at[away - 1, group], recv_sem=t_recv.at[away - 1, group],
            device_id=cross(away), device_id_type=MESH,
        )

    def landed(slot, group):
        at = pl.ds(48 * group, 48)
        return pltpu.make_async_remote_copy(
            src_ref=codes.at[0, at], dst_ref=far.at[slot, at],
            send_sem=t_send.at[slot, group], recv_sem=t_recv.at[slot, group],
            device_id=cross(slot + 1), device_id_type=MESH,
        )

    for group, pieces in enumerate(GROUPS):
        for piece in pieces:
            lo, hi = PIECES[piece]
            hop(RIGHT, 3, piece).wait_recv()
            hop(LEFT, 3, piece).wait_recv()
            sums[lo:hi, :] = (
                gram[7, lo:hi, :] + decode(got[RIGHT, 3, lo:hi, :]) + decode(got[LEFT, 3, lo:hi, :])
            )
        if 2 in pieces:
            for k in range(4):
                rest[48 * k:48 * (k + 1), 0:REST] = sums[TAIL:TAIL + 48, REST * k:REST * (k + 1)]
        for to in range(SIDE):
            parts = []
            for tile in COLUMNS[group]:
                if tile < FULL:
                    at = TILES[tile] + ROWS * to
                    parts.append(sums[at:at + 24, :])
                else:
                    parts.append(rest[ROWS * to:ROWS * to + 24, :])
            both = jnp.concatenate(parts, 0)
            flat[to, 48 * group:48 * group + 48, :] = both
            codes[to, 48 * group:48 * group + 48, :] = encode(both)
        for number in range(SIDE - 1):
            over(number, group).start()

    load_f.wait()
    theirs = jnp.zeros((48, HALF), jnp.float32)
    mine = jnp.zeros((48, HALF), jnp.float32)
    for group in range(3):
        total = flat[across, 48 * group:48 * group + 48, :]
        for slot in range(SIDE - 1):
            landed(slot, group).wait_recv()
            total += decode(far[slot, 48 * group:48 * group + 48, :])
        both = []
        for k, (lo, hi) in enumerate(spans(group)):
            new = decay_rate * fac[:, lo:hi] + scale_new * total[24 * k:24 * k + ROWS, 0:hi - lo]
            f_out[:, lo:hi] = new
            new = jnp.concatenate([new, jnp.zeros((24 - ROWS, hi - lo), jnp.float32)], 0)
            high = new.astype(jnp.bfloat16).astype(jnp.float32)
            both.append(jnp.concatenate([high, new - high], 0).astype(jnp.bfloat16))
        theirs += turned(both, base_hi, base_lo, not_core, group)
        if group < 2:
            mine += turned(both, base_hi, base_lo, core, group)

    prod[...] = theirs[0:24] + theirs[24:48]
    give_r = pltpu.make_async_remote_copy(
        src_ref=prod, dst_ref=prod_got, send_sem=p_send, recv_sem=p_recv,
        device_id=partner, device_id_type=MESH,
    )
    give_r.start()
    mine += turned(both, base_hi, base_lo, core, 2)
    for way in range(2):
        for step in range(4):
            for piece in range(5):
                if rows_of(way, step, piece) is not None:
                    hop(way, step, piece).wait_send()
    for number in range(SIDE - 1):
        for group in range(3):
            over(number, group).wait_send()
    give_r.wait()
    r_out[...] = mine[0:ROWS] + mine[24:24 + ROWS] + prod_got[0:ROWS, :]


def shards(tokens, factor_old, basis):
    tok_rows, features = tokens.shape
    scale_new = (1.0 - decay_rate) / (tok_rows * lax.axis_size("dp"))
    f32, bf16 = jnp.float32, jnp.bfloat16
    body = lambda *refs: kernel(scale_new, *refs)
    dma = pltpu.SemaphoreType.DMA
    return pl.pallas_call(
        body,
        name="gram_rotate",
        out_shape=(
            jax.ShapeDtypeStruct((ROWS, HALF), f32),
            jax.ShapeDtypeStruct((ROWS, HALF), f32),
        ),
        in_specs=[pl.BlockSpec(memory_space=pl.ANY)] * 3,
        out_specs=[pl.BlockSpec(memory_space=pltpu.VMEM)] * 2,
        scratch_shapes=[
            pltpu.VMEM((HALF, tok_rows), bf16),
            pltpu.VMEM((HALF, tok_rows), bf16),
            pltpu.VMEM((2 * HALF + 8, tok_rows), f32),
            pltpu.VMEM((192, tok_rows), f32),
            pltpu.VMEM((SIDE, LONG, 128), f32),
            pltpu.VMEM((LONG, 128), f32),
            pltpu.VMEM((192, 128), f32),
            pltpu.VMEM((2, 4, LONG, 128), bf16),
            pltpu.VMEM((2, 4, LONG, 128), bf16),
            pltpu.VMEM((SIDE, 144, 128), f32),
            pltpu.VMEM((SIDE, 144, 128), bf16),
            pltpu.VMEM((SIDE - 1, 144, 128), bf16),
            pltpu.VMEM((ROWS, HALF), f32),
            pltpu.VMEM((HALF, 2 * HALF), f32),
            pltpu.VMEM((2, HALF, HALF), bf16),
            pltpu.VMEM((2, HALF, HALF), bf16),
            pltpu.VMEM((24, HALF), f32),
            pltpu.VMEM((24, HALF), f32),
            dma((3,)),
            dma((2,)),
            dma((2, 4, 5)),
            dma((2, 4, 5)),
            dma((SIDE - 1, 3)),
            dma((SIDE - 1, 3)),
            dma,
            dma,
            pltpu.SemaphoreType.REGULAR((3,)),
        ],
        compiler_params=pltpu.CompilerParams(
            collective_id=0, has_side_effects=True, vmem_limit_bytes=55040 * 1024
        ),
    )(tokens.T, factor_old, basis)


def solution(mesh):
    return jax.shard_map(
        shards,
        mesh=mesh,
        in_specs=(P("dp", "mp"), P("dp", "mp"), P("mp", None)),
        out_specs=(P("dp", "mp"), P("dp", "mp")),
        check_vma=False,
    )
```

```python
import jax
import jax.numpy as jnp
from jax import lax
from jax.experimental import pallas as pl
from jax.experimental.pallas import tpu as pltpu
from jax.sharding import PartitionSpec as P

decay_rate = 0.95

MESH = pl.DeviceIdType.MESH
SIDE = 8
ROWS = 21
CHUNK = SIDE * ROWS
HALF = 672
FULL = 5
REST = HALF - 128 * FULL
TILES = (0, CHUNK, 2 * CHUNK, 3 * CHUNK + 56, 4 * CHUNK + 56)
TAIL = 3 * CHUNK
LONG = 5 * CHUNK + 56
PIECES = ((0, 176), (176, 336), (336, 560), (560, 720), (720, LONG))
SUBS = ((0, 176), (176, 336), (336, 448), (448, 560), (560, 720), (720, LONG))
SUBS_OF = ((0,), (1,), (2, 3), (4,), (5,))
GROUPS = ((0, 1), (3, 4), (2,))
COLUMNS = ((0, 1), (3, 4), (2, 5))
RIGHT, LEFT = 0, 1
FAR = (4, 3, 5)
NEAR = (2, 6, 1, 7)
FIRST = (0, 1)


def encode(value):
    return ((value * jnp.abs(value)) * (value * value)).astype(jnp.bfloat16)


def decode(code):
    code = code.astype(jnp.float32)
    root = lax.rsqrt(lax.rsqrt(jnp.abs(code)))
    return jnp.where(code < 0.0, -root, root)


def spans(group):
    return [(128 * tile, min(128 * tile + 128, HALF)) for tile in COLUMNS[group]]


def turned(both, base_hi, base_lo, half, group):
    out = jnp.zeros((48, HALF), jnp.float32)
    for part, (lo, hi) in zip(both, spans(group)):
        out += jnp.dot(part, base_hi[half, lo:hi, :], preferred_element_type=jnp.float32)
        out += jnp.dot(part, base_lo[half, lo:hi, :], preferred_element_type=jnp.float32)
    return out


def kernel(
    scale_new, tok, old, bas, f_out, r_out,
    own_x, par_x, wide_x, left_x, gram, sums, rest, sent0, got0, sent, got, flat, codes, far, fac,
    base, base_hi, base_lo, prod, prod_got,
    load_sem, par_sem, z_send, z_recv, s_send, s_recv, t_send, t_recv, w_send, w_recv,
    p_send, p_recv, ready, hello, go,
):
    dp, mp = lax.axis_index("dp"), lax.axis_index("mp")
    y, z, core = dp // SIDE, dp % SIDE, mp % 2
    not_core = 1 - core
    here = not_core * y + core * z
    across = core * y + not_core * z

    def along(step):
        to_y = (y + not_core * step + SIDE) % SIDE
        to_z = (z + core * step + SIDE) % SIDE
        return {"dp": to_y * SIDE + to_z, "mp": mp}

    def cross(step):
        to_y = (y + core * step + SIDE) % SIDE
        to_z = (z + not_core * step + SIDE) % SIDE
        return {"dp": to_y * SIDE + to_z, "mp": mp}

    partner = {"dp": dp, "mp": mp + 1 - 2 * core}

    load_x = pltpu.make_async_copy(tok, own_x, load_sem.at[0])
    load_b = pltpu.make_async_copy(bas, base, load_sem.at[1])
    load_f = pltpu.make_async_copy(old, fac, load_sem.at[2])
    load_x.start()
    barrier = pltpu.get_barrier_semaphore()
    for step in (1, -1):
        for to_y, to_z in (((y + step + SIDE) % SIDE, z), (y, (z + step + SIDE) % SIDE)):
            pl.semaphore_signal(
                barrier, inc=1, device_id={"dp": to_y * SIDE + to_z, "mp": mp - core},
                device_id_type=MESH,
            )
    give_x = pltpu.make_async_remote_copy(
        src_ref=tok, dst_ref=par_x, send_sem=par_sem.at[0], recv_sem=par_sem.at[1],
        device_id=partner, device_id_type=MESH,
    )

    @pl.when(core == 1)
    def _():
        pl.semaphore_wait(barrier, 1)
        pl.semaphore_signal(hello, inc=1, device_id=partner, device_id_type=MESH)
        give_x.start()

    @pl.when(core == 0)
    def _():
        pl.semaphore_signal(barrier, inc=1, device_id=partner, device_id_type=MESH)
        pl.semaphore_wait(hello, 1)
        give_x.start()

    load_b.start()
    load_f.start()
    wide_x[2 * HALF:2 * HALF + 8, :] = jnp.zeros((8, wide_x.shape[1]), jnp.float32)
    left_x[CHUNK:192, :] = jnp.zeros((192 - CHUNK, wide_x.shape[1]), jnp.float32)
    sums[LONG:LONG + 8, :] = jnp.zeros((8, 128), jnp.float32)
    for slot in range(SIDE):
        gram[slot, TAIL + 48:TAIL + 56, :] = jnp.zeros((8, 128), jnp.float32)

    def announce(number):
        for device in (cross(1), cross(-1)):
            pl.semaphore_signal(
                ready.at[number], inc=1, device_id=device, device_id_type=MESH
            )

    load_x.wait()
    wide_x[pl.ds(pl.multiple_of(HALF * core, 8), HALF), :] = own_x[...].astype(jnp.float32)
    give_x.wait_recv()
    wide_x[pl.ds(pl.multiple_of(HALF * not_core, 8), HALF), :] = par_x[...].astype(jnp.float32)

    def products(slot, position):
        for group in range(SIDE):
            in_y = CHUNK * position + ROWS * group
            in_z = ROWS * position + CHUNK * group
            start = not_core * in_y + core * in_z
            block = wide_x[pl.ds(pl.multiple_of(start // 8 * 8, 8), 32), :]
            block = pltpu.roll(block, (32 - start % 8) % 32, 0)
            left_x[ROWS * group:ROWS * group + 24, :] = block[0:24]
        left = left_x[...].astype(jnp.bfloat16)
        main = lax.dot_general(
            left[0:176], own_x[0:128 * FULL, :], (((1,), (1,)), ((), ())),
            preferred_element_type=jnp.float32,
        )
        for tile in range(FULL):
            gram[slot, TILES[tile]:TILES[tile] + CHUNK, :] = main[0:CHUNK, 128 * tile:128 * (tile + 1)]
        thin = lax.dot_general(
            left, own_x[128 * FULL:HALF, :], (((1,), (1,)), ((), ())),
            preferred_element_type=jnp.float32,
        )
        gram[slot, TAIL:TAIL + 48, :] = jnp.concatenate(
            [thin[48 * k:48 * (k + 1)] for k in range(4)], 1
        )

    def slot_of(way, step):
        return 0 if step == 0 else 2 * step - 1 + way

    def hop0(way, sub):
        lo, hi = SUBS[sub]
        return pltpu.make_async_remote_copy(
            src_ref=sent0.at[pl.ds(lo, hi - lo)], dst_ref=got0.at[pl.ds(lo, hi - lo)],
            send_sem=z_send.at[sub], recv_sem=z_recv.at[sub],
            device_id=along(1 if way == RIGHT else -1), device_id_type=MESH,
        )

    def hop(way, step, piece):
        lo, hi = PIECES[piece]
        return pltpu.make_async_remote_copy(
            src_ref=sent.at[way, step - 1, pl.ds(lo, hi - lo)],
            dst_ref=got.at[way, step - 1, pl.ds(lo, hi - lo)],
            send_sem=s_send.at[way, step - 1, piece], recv_sem=s_recv.at[way, step - 1, piece],
            device_id=along(1 if way == RIGHT else -1), device_id_type=MESH,
        )

    def put(way, step, piece, first=()):
        slot = slot_of(way, step)
        lo, hi = PIECES[piece]
        if step == 1:
            for sub in SUBS_OF[piece]:
                a, b = SUBS[sub]
                total = gram[slot, a:b, :]
                if sub in first:
                    hop0(way, sub).wait_recv()
                    total = total + decode(got0[a:b, :])
                sent[way, 0, a:b, :] = encode(total)
        else:
            hop(way, step - 1, piece).wait_recv()
            sent[way, step - 1, lo:hi, :] = encode(
                gram[slot, lo:hi, :] + decode(got[way, step - 2, lo:hi, :])
            )
        hop(way, step, piece).start()

    def split_base(first, last):
        @pl.loop(first, last)
        def _(part):
            at = pl.ds(pl.multiple_of(part * 96, 96), 96)
            for half in range(2):
                value = base[at, HALF * half:HALF * (half + 1)]
                high = value.astype(jnp.bfloat16)
                base_hi[half, at, :] = high
                base_lo[half, at, :] = (value - high.astype(jnp.float32)).astype(jnp.bfloat16)

    every = (0, 1, 3, 4, 2)
    ahead = ((3, 4, 0, 1, 2), (1, 0, 4, 3, 2))

    products(0, (here + 4) % SIDE)
    sent0[...] = encode(gram[0])

    @pl.when(core == 0)
    def _():
        pl.semaphore_wait(barrier, 8)
        pl.semaphore_signal(go, inc=1, device_id=partner, device_id_type=MESH)
        for right, left in ((0, 5), (1, 4), (2, 3)):
            hop0(RIGHT, right).start()
            hop0(LEFT, left).start()

    @pl.when(core == 1)
    def _():
        pl.semaphore_wait(go, 1)
        for sub in (0, 1, 4, 5, 2, 3):
            hop0(LEFT, sub).start()

    announce(0)
    products(1, (here + 3) % SIDE)
    products(2, (here + 5) % SIDE)

    @pl.when(core == 0)
    def _():
        for place in (0, 1):
            put(RIGHT, 1, ahead[RIGHT][place])
            put(LEFT, 1, ahead[LEFT][place])

    @pl.when(core == 1)
    def _():
        for piece in every:
            put(RIGHT, 1, piece)

    products(3, (here + 2) % SIDE)
    products(4, (here + 6) % SIDE)

    @pl.when(core == 0)
    def _():
        for place in (2, 3, 4):
            put(RIGHT, 1, ahead[RIGHT][place], (0, 1, 2))
            put(LEFT, 1, ahead[LEFT][place], (3, 4, 5))

    @pl.when(core == 1)
    def _():
        for piece in every:
            put(RIGHT, 2, piece)
            put(LEFT, 1, piece, range(6))

    pl.semaphore_wait(ready.at[0], 2)
    announce(1)
    products(5, (here + 1) % SIDE)
    products(6, (here + 7) % SIDE)

    @pl.when(core == 0)
    def _():
        for place in range(5):
            put(RIGHT, 2, ahead[RIGHT][place])
            put(LEFT, 2, ahead[LEFT][place])

    @pl.when(core == 1)
    def _():
        for piece in every:
            put(RIGHT, 3, piece)
            put(LEFT, 2, piece)

    pl.semaphore_wait(ready.at[1], 2)
    announce(2)
    products(7, here)
    load_b.wait()
    split_base(0, 4)

    @pl.when(core == 0)
    def _():
        for place in range(5):
            put(RIGHT, 3, ahead[RIGHT][place])
            put(LEFT, 3, ahead[LEFT][place])

    @pl.when(core == 1)
    def _():
        for piece in every:
            put(LEFT, 3, piece)

    split_base(4, 7)
    pl.semaphore_wait(ready.at[2], 2)

    def over(to, group):
        away = (to - across + SIDE) % SIDE
        slot = away - 1
        if group is None:
            at, send, recv = pl.ds(0, 144), w_send.at[slot], w_recv.at[slot]
        else:
            at, send, recv = pl.ds(48 * group, 48), t_send.at[slot, group], t_recv.at[slot, group]
        return pltpu.make_async_remote_copy(
            src_ref=codes.at[to, at], dst_ref=far.at[slot, at], send_sem=send, recv_sem=recv,
            device_id=cross(away), device_id_type=MESH,
        )

    def each_over(group, act):
        @pl.when(core == 0)
        def _():
            for to in range(SIDE):
                if (to in FIRST) == (group is not None):
                    @pl.when(across != to)
                    def _():
                        act(over(to, group))

        @pl.when(core == 1)
        def _():
            for step in NEAR if group is None else FAR:
                act(over((across + step) % SIDE, group))

    def landed(group):
        def one(step):
            over((across + step) % SIDE, group).wait_recv()

        def whole(step):
            if group == 0:
                over((across + step) % SIDE, None).wait_recv()

        @pl.when(core == 1)
        def _():
            for step in FAR:
                one(step)
            for step in NEAR:
                whole(step)

        @pl.when((core == 0) & (across < len(FIRST)))
        def _():
            for step in range(1, SIDE):
                one(step)

        @pl.when((core == 0) & (across >= len(FIRST)))
        def _():
            for step in range(1, SIDE):
                whole(step)

    for group, pieces in enumerate(GROUPS):
        for piece in pieces:
            lo, hi = PIECES[piece]
            hop(RIGHT, 3, piece).wait_recv()
            hop(LEFT, 3, piece).wait_recv()
            sums[lo:hi, :] = (
                gram[7, lo:hi, :] + decode(got[RIGHT, 2, lo:hi, :]) + decode(got[LEFT, 2, lo:hi, :])
            )
        if 2 in pieces:
            for k in range(4):
                rest[48 * k:48 * (k + 1), 0:REST] = sums[TAIL:TAIL + 48, REST * k:REST * (k + 1)]
        for to in range(SIDE):
            parts = []
            for tile in COLUMNS[group]:
                if tile < FULL:
                    at = TILES[tile] + ROWS * to
                    parts.append(sums[at:at + 24, :])
                else:
                    parts.append(rest[ROWS * to:ROWS * to + 24, :])
            both = jnp.concatenate(parts, 0)
            flat[to, 48 * group:48 * group + 48, :] = both
            codes[to, 48 * group:48 * group + 48, :] = encode(both)
        each_over(group, lambda copy: copy.start())
    each_over(None, lambda copy: copy.start())

    load_f.wait()
    theirs = jnp.zeros((48, HALF), jnp.float32)
    mine = jnp.zeros((48, HALF), jnp.float32)
    for group in range(3):
        total = flat[across, 48 * group:48 * group + 48, :]
        landed(group)
        for slot in range(SIDE - 1):
            total += decode(far[slot, 48 * group:48 * group + 48, :])
        both = []
        for k, (lo, hi) in enumerate(spans(group)):
            new = decay_rate * fac[:, lo:hi] + scale_new * total[24 * k:24 * k + ROWS, 0:hi - lo]
            f_out[:, lo:hi] = new
            new = jnp.concatenate([new, jnp.zeros((24 - ROWS, hi - lo), jnp.float32)], 0)
            high = new.astype(jnp.bfloat16).astype(jnp.float32)
            both.append(jnp.concatenate([high, new - high], 0).astype(jnp.bfloat16))
        theirs += turned(both, base_hi, base_lo, not_core, group)
        if group < 2:
            mine += turned(both, base_hi, base_lo, core, group)

    prod[...] = theirs[0:24] + theirs[24:48]
    give_r = pltpu.make_async_remote_copy(
        src_ref=prod, dst_ref=prod_got, send_sem=p_send, recv_sem=p_recv,
        device_id=partner, device_id_type=MESH,
    )
    give_r.start()
    mine += turned(both, base_hi, base_lo, core, 2)
    give_x.wait_send()

    @pl.when(core == 0)
    def _():
        for sub in range(6):
            hop0(RIGHT if sub < 3 else LEFT, sub).wait_send()

    @pl.when(core == 1)
    def _():
        for sub in range(6):
            hop0(LEFT, sub).wait_send()

    for way in range(2):
        for step in (1, 2, 3):
            for piece in range(5):
                hop(way, step, piece).wait_send()
    for group in (0, 1, 2, None):
        each_over(group, lambda copy: copy.wait_send())
    give_r.wait()
    r_out[...] = mine[0:ROWS] + mine[24:24 + ROWS] + prod_got[0:ROWS, :]


def shards(tokens, factor_old, basis):
    tok_rows, features = tokens.shape
    scale_new = (1.0 - decay_rate) / (tok_rows * lax.axis_size("dp"))
    f32, bf16 = jnp.float32, jnp.bfloat16
    body = lambda *refs: kernel(scale_new, *refs)
    dma = pltpu.SemaphoreType.DMA
    return pl.pallas_call(
        body,
        name="gram_rotate",
        out_shape=(
            jax.ShapeDtypeStruct((ROWS, HALF), f32),
            jax.ShapeDtypeStruct((ROWS, HALF), f32),
        ),
        in_specs=[pl.BlockSpec(memory_space=pl.ANY)] * 3,
        out_specs=[pl.BlockSpec(memory_space=pltpu.VMEM)] * 2,
        scratch_shapes=[
            pltpu.VMEM((HALF, tok_rows), bf16),
            pltpu.VMEM((HALF, tok_rows), bf16),
            pltpu.VMEM((2 * HALF + 8, tok_rows), f32),
            pltpu.VMEM((192, tok_rows), f32),
            pltpu.VMEM((SIDE, LONG, 128), f32),
            pltpu.VMEM((LONG + 8, 128), f32),
            pltpu.VMEM((192, 128), f32),
            pltpu.VMEM((LONG, 128), bf16),
            pltpu.VMEM((LONG, 128), bf16),
            pltpu.VMEM((2, 3, LONG, 128), bf16),
            pltpu.VMEM((2, 3, LONG, 128), bf16),
            pltpu.VMEM((SIDE, 144, 128), f32),
            pltpu.VMEM((SIDE, 144, 128), bf16),
            pltpu.VMEM((SIDE - 1, 144, 128), bf16),
            pltpu.VMEM((ROWS, HALF), f32),
            pltpu.VMEM((HALF, 2 * HALF), f32),
            pltpu.VMEM((2, HALF, HALF), bf16),
            pltpu.VMEM((2, HALF, HALF), bf16),
            pltpu.VMEM((24, HALF), f32),
            pltpu.VMEM((24, HALF), f32),
            dma((3,)),
            dma((2,)),
            dma((6,)),
            dma((6,)),
            dma((2, 3, 5)),
            dma((2, 3, 5)),
            dma((SIDE - 1, 3)),
            dma((SIDE - 1, 3)),
            dma((SIDE - 1,)),
            dma((SIDE - 1,)),
            dma,
            dma,
            pltpu.SemaphoreType.REGULAR((3,)),
            pltpu.SemaphoreType.REGULAR,
            pltpu.SemaphoreType.REGULAR,
        ],
        compiler_params=pltpu.CompilerParams(
            collective_id=0, has_side_effects=True, vmem_limit_bytes=55040 * 1024
        ),
    )(tokens.T, factor_old, basis)


def solution(mesh):
    return jax.shard_map(
        shards,
        mesh=mesh,
        in_specs=(P("dp", "mp"), P("dp", "mp"), P("mp", None)),
        out_specs=(P("dp", "mp"), P("dp", "mp")),
        check_vma=False,
    )
```

```python
import jax
import jax.numpy as jnp
from jax import lax
from jax.experimental import pallas as pl
from jax.experimental.pallas import tpu as pltpu
from jax.sharding import PartitionSpec as P

decay_rate = 0.95

MESH = pl.DeviceIdType.MESH
SIDE = 8
ROWS = 21
CHUNK = SIDE * ROWS
HALF = 672
FULL = 5
REST = HALF - 128 * FULL
TILES = (0, CHUNK, 2 * CHUNK, 3 * CHUNK + 56, 4 * CHUNK + 56)
TAIL = 3 * CHUNK
LONG = 5 * CHUNK + 56
PIECES = ((0, 176), (176, 336), (336, 560), (560, 720), (720, LONG))
SUBS = ((0, 176), (176, 336), (336, 448), (448, 560), (560, 720), (720, LONG))
SUBS_OF = ((0,), (1,), (2, 3), (4,), (5,))
GROUPS = ((0, 1), (3, 4), (2,))
COLUMNS = ((0, 1), (3, 4), (2, 5))
RIGHT, LEFT = 0, 1
FAR = (4, 3, 5)
NEAR = (2, 6, 1, 7)
FIRST = (0, 1)


def encode(value):
    return ((value * jnp.abs(value)) * (value * value)).astype(jnp.bfloat16)


def decode(code):
    code = code.astype(jnp.float32)
    root = lax.rsqrt(lax.rsqrt(jnp.abs(code)))
    return jnp.where(code < 0.0, -root, root)


def spans(group):
    return [(128 * tile, min(128 * tile + 128, HALF)) for tile in COLUMNS[group]]


def turned(both, base_hi, base_lo, half, group):
    out = jnp.zeros((48, HALF), jnp.float32)
    for part, (lo, hi) in zip(both, spans(group)):
        out += jnp.dot(part, base_hi[half, lo:hi, :], preferred_element_type=jnp.float32)
        out += jnp.dot(part, base_lo[half, lo:hi, :], preferred_element_type=jnp.float32)
    return out


def kernel(
    scale_new, tok, old, bas, f_out, r_out,
    own_x, par_x, wide_x, left_x, gram, sums, rest, sent0, got0, sent, got, flat, codes, far, fac,
    base, base_hi, base_lo, prod, prod_got,
    load_sem, par_sem, z_send, z_recv, s_send, s_recv, t_send, t_recv,
    p_send, p_recv, ready, hello, go,
):
    dp, mp = lax.axis_index("dp"), lax.axis_index("mp")
    y, z, core = dp // SIDE, dp % SIDE, mp % 2
    not_core = 1 - core
    here = not_core * y + core * z
    across = core * y + not_core * z

    def along(step):
        to_y = (y + not_core * step + SIDE) % SIDE
        to_z = (z + core * step + SIDE) % SIDE
        return {"dp": to_y * SIDE + to_z, "mp": mp}

    def cross(step):
        to_y = (y + core * step + SIDE) % SIDE
        to_z = (z + not_core * step + SIDE) % SIDE
        return {"dp": to_y * SIDE + to_z, "mp": mp}

    partner = {"dp": dp, "mp": mp + 1 - 2 * core}

    load_x = pltpu.make_async_copy(tok, own_x, load_sem.at[0])
    load_b = pltpu.make_async_copy(bas, base, load_sem.at[1])
    load_f = pltpu.make_async_copy(old, fac, load_sem.at[2])
    load_x.start()
    barrier = pltpu.get_barrier_semaphore()
    for step in (1, -1):
        for to_y, to_z in (((y + step + SIDE) % SIDE, z), (y, (z + step + SIDE) % SIDE)):
            pl.semaphore_signal(
                barrier, inc=1, device_id={"dp": to_y * SIDE + to_z, "mp": mp - core},
                device_id_type=MESH,
            )
    give_x = pltpu.make_async_remote_copy(
        src_ref=tok, dst_ref=par_x, send_sem=par_sem.at[0], recv_sem=par_sem.at[1],
        device_id=partner, device_id_type=MESH,
    )

    @pl.when(core == 1)
    def _():
        pl.semaphore_wait(barrier, 1)
        pl.semaphore_signal(hello, inc=1, device_id=partner, device_id_type=MESH)
        give_x.start()

    @pl.when(core == 0)
    def _():
        pl.semaphore_signal(barrier, inc=1, device_id=partner, device_id_type=MESH)
        pl.semaphore_wait(hello, 1)
        give_x.start()

    load_b.start()
    load_f.start()
    wide_x[2 * HALF:2 * HALF + 8, :] = jnp.zeros((8, wide_x.shape[1]), jnp.float32)
    left_x[CHUNK:192, :] = jnp.zeros((192 - CHUNK, wide_x.shape[1]), jnp.float32)
    sums[LONG:LONG + 8, :] = jnp.zeros((8, 128), jnp.float32)
    for slot in range(SIDE):
        gram[slot, TAIL + 48:TAIL + 56, :] = jnp.zeros((8, 128), jnp.float32)

    def announce(number):
        for device in (cross(1), cross(-1)):
            pl.semaphore_signal(
                ready.at[number], inc=1, device_id=device, device_id_type=MESH
            )

    load_x.wait()
    wide_x[pl.ds(pl.multiple_of(HALF * core, 8), HALF), :] = own_x[...].astype(jnp.float32)
    alone = (core == 0) & (y >= SIDE // 2)

    def take_x():
        give_x.wait_recv()
        wide_x[pl.ds(pl.multiple_of(HALF * not_core, 8), HALF), :] = par_x[...].astype(jnp.float32)

    pl.when(jnp.logical_not(alone))(take_x)

    def products(slot, position):
        for group in range(SIDE):
            in_y = CHUNK * position + ROWS * group
            in_z = ROWS * position + CHUNK * group
            start = not_core * in_y + core * in_z
            block = wide_x[pl.ds(pl.multiple_of(start // 8 * 8, 8), 32), :]
            block = pltpu.roll(block, (32 - start % 8) % 32, 0)
            left_x[ROWS * group:ROWS * group + 24, :] = block[0:24]
        left = left_x[...].astype(jnp.bfloat16)
        main = lax.dot_general(
            left[0:176], own_x[0:128 * FULL, :], (((1,), (1,)), ((), ())),
            preferred_element_type=jnp.float32,
        )
        for tile in range(FULL):
            gram[slot, TILES[tile]:TILES[tile] + CHUNK, :] = main[0:CHUNK, 128 * tile:128 * (tile + 1)]
        thin = lax.dot_general(
            left, own_x[128 * FULL:HALF, :], (((1,), (1,)), ((), ())),
            preferred_element_type=jnp.float32,
        )
        gram[slot, TAIL:TAIL + 48, :] = jnp.concatenate(
            [thin[48 * k:48 * (k + 1)] for k in range(4)], 1
        )

    def slot_of(way, step):
        return 0 if step == 0 else 2 * step - 1 + way

    def hop0(way, sub):
        lo, hi = SUBS[sub]
        return pltpu.make_async_remote_copy(
            src_ref=sent0.at[pl.ds(lo, hi - lo)], dst_ref=got0.at[pl.ds(lo, hi - lo)],
            send_sem=z_send.at[sub], recv_sem=z_recv.at[sub],
            device_id=along(1 if way == RIGHT else -1), device_id_type=MESH,
        )

    def hop(way, step, piece):
        lo, hi = PIECES[piece]
        return pltpu.make_async_remote_copy(
            src_ref=sent.at[way, step - 1, pl.ds(lo, hi - lo)],
            dst_ref=got.at[way, step - 1, pl.ds(lo, hi - lo)],
            send_sem=s_send.at[way, step - 1, piece], recv_sem=s_recv.at[way, step - 1, piece],
            device_id=along(1 if way == RIGHT else -1), device_id_type=MESH,
        )

    def put(way, step, piece, first=()):
        slot = slot_of(way, step)
        lo, hi = PIECES[piece]
        if step == 1:
            for sub in SUBS_OF[piece]:
                a, b = SUBS[sub]
                total = gram[slot, a:b, :]
                if sub in first:
                    hop0(way, sub).wait_recv()
                    total = total + decode(got0[a:b, :])
                sent[way, 0, a:b, :] = encode(total)
        else:
            hop(way, step - 1, piece).wait_recv()
            sent[way, step - 1, lo:hi, :] = encode(
                gram[slot, lo:hi, :] + decode(got[way, step - 2, lo:hi, :])
            )
        hop(way, step, piece).start()

    def split_base(first, last):
        @pl.loop(first, last)
        def _(part):
            at = pl.ds(pl.multiple_of(part * 96, 96), 96)
            for half in range(2):
                value = base[at, HALF * half:HALF * (half + 1)]
                high = value.astype(jnp.bfloat16)
                base_hi[half, at, :] = high
                base_lo[half, at, :] = (value - high.astype(jnp.float32)).astype(jnp.bfloat16)

    every = (0, 1, 3, 4, 2)
    ahead = ((3, 4, 0, 1, 2), (1, 0, 4, 3, 2))

    def first_chunk():
        products(0, (here + 4) % SIDE)
        sent0[...] = encode(gram[0])

    @pl.when(core == 0)
    def _():
        first_chunk()
        pl.semaphore_wait(barrier, 8)
        pl.semaphore_signal(go, inc=1, device_id=partner, device_id_type=MESH)
        for right, left in ((0, 5), (1, 4), (2, 3)):
            hop0(RIGHT, right).start()
            hop0(LEFT, left).start()

    @pl.when(core == 1)
    def _():
        products(1, (here + 3) % SIDE)
        pl.semaphore_wait(go, 1)
        for piece in every:
            put(RIGHT, 1, piece)
        first_chunk()
        for sub in (0, 1, 4, 5, 2, 3):
            hop0(LEFT, sub).start()

    pl.when(alone)(take_x)
    announce(0)

    @pl.when(core == 0)
    def _():
        products(1, (here + 3) % SIDE)

    products(2, (here + 5) % SIDE)

    @pl.when(core == 0)
    def _():
        for place in (0, 1):
            put(RIGHT, 1, ahead[RIGHT][place])
            put(LEFT, 1, ahead[LEFT][place])

    products(3, (here + 2) % SIDE)
    products(4, (here + 6) % SIDE)

    @pl.when(core == 0)
    def _():
        for place in (2, 3, 4):
            put(RIGHT, 1, ahead[RIGHT][place], (0, 1, 2))
            put(LEFT, 1, ahead[LEFT][place], (3, 4, 5))

    @pl.when(core == 1)
    def _():
        for piece in every:
            put(RIGHT, 2, piece)
            put(LEFT, 1, piece, range(6))

    pl.semaphore_wait(ready.at[0], 2)
    announce(1)
    products(5, (here + 1) % SIDE)
    products(6, (here + 7) % SIDE)

    @pl.when(core == 0)
    def _():
        for place in range(5):
            put(RIGHT, 2, ahead[RIGHT][place])
            put(LEFT, 2, ahead[LEFT][place])

    @pl.when(core == 1)
    def _():
        for piece in every:
            put(RIGHT, 3, piece)
            put(LEFT, 2, piece)

    pl.semaphore_wait(ready.at[1], 2)
    announce(2)
    products(7, here)
    load_b.wait()
    split_base(0, 4)

    @pl.when(core == 0)
    def _():
        for place in range(5):
            put(RIGHT, 3, ahead[RIGHT][place])
            put(LEFT, 3, ahead[LEFT][place])

    @pl.when(core == 1)
    def _():
        for piece in every:
            put(LEFT, 3, piece)

    split_base(4, 7)
    pl.semaphore_wait(ready.at[2], 2)

    PAIR = 3

    def over(to, group):
        away = (to - across + SIDE) % SIDE
        slot = away - 1
        at = pl.ds(0, 96) if group == PAIR else pl.ds(48 * group, 48)
        return pltpu.make_async_remote_copy(
            src_ref=codes.at[to, at], dst_ref=far.at[slot, at],
            send_sem=t_send.at[slot, group], recv_sem=t_recv.at[slot, group],
            device_id=cross(away), device_id_type=MESH,
        )

    def each_over(group, act):
        def send(to, single):
            if single or group == 2:
                act(over(to, group))
            elif group == 1:
                act(over(to, PAIR))

        @pl.when(core == 0)
        def _():
            for to in range(SIDE):
                @pl.when(across != to)
                def _():
                    send(to, to in FIRST)

        @pl.when(core == 1)
        def _():
            for step in FAR:
                send((across + step) % SIDE, True)
            for step in NEAR:
                send((across + step) % SIDE, False)

    def landed(group):
        def one(step, single):
            if single or group == 2:
                over((across + step) % SIDE, group).wait_recv()
            elif group == 0:
                over((across + step) % SIDE, PAIR).wait_recv()

        @pl.when(core == 1)
        def _():
            for step in FAR:
                one(step, True)
            for step in NEAR:
                one(step, False)

        @pl.when((core == 0) & (across < len(FIRST)))
        def _():
            for step in range(1, SIDE):
                one(step, True)

        @pl.when((core == 0) & (across >= len(FIRST)))
        def _():
            for step in range(1, SIDE):
                one(step, False)

    for group, pieces in enumerate(GROUPS):
        for piece in pieces:
            lo, hi = PIECES[piece]
            hop(RIGHT, 3, piece).wait_recv()
            hop(LEFT, 3, piece).wait_recv()
            sums[lo:hi, :] = (
                gram[7, lo:hi, :] + decode(got[RIGHT, 2, lo:hi, :]) + decode(got[LEFT, 2, lo:hi, :])
            )
        if 2 in pieces:
            for k in range(4):
                rest[48 * k:48 * (k + 1), 0:REST] = sums[TAIL:TAIL + 48, REST * k:REST * (k + 1)]
        for to in range(SIDE):
            parts = []
            for tile in COLUMNS[group]:
                if tile < FULL:
                    at = TILES[tile] + ROWS * to
                    parts.append(sums[at:at + 24, :])
                else:
                    parts.append(rest[ROWS * to:ROWS * to + 24, :])
            both = jnp.concatenate(parts, 0)
            flat[to, 48 * group:48 * group + 48, :] = both
            codes[to, 48 * group:48 * group + 48, :] = encode(both)
        each_over(group, lambda copy: copy.start())

    load_f.wait()
    theirs = jnp.zeros((48, HALF), jnp.float32)
    mine = jnp.zeros((48, HALF), jnp.float32)
    for group in range(3):
        total = flat[across, 48 * group:48 * group + 48, :]
        landed(group)
        for slot in range(SIDE - 1):
            total += decode(far[slot, 48 * group:48 * group + 48, :])
        both = []
        for k, (lo, hi) in enumerate(spans(group)):
            new = decay_rate * fac[:, lo:hi] + scale_new * total[24 * k:24 * k + ROWS, 0:hi - lo]
            f_out[:, lo:hi] = new
            new = jnp.concatenate([new, jnp.zeros((24 - ROWS, hi - lo), jnp.float32)], 0)
            high = new.astype(jnp.bfloat16).astype(jnp.float32)
            both.append(jnp.concatenate([high, new - high], 0).astype(jnp.bfloat16))
        theirs += turned(both, base_hi, base_lo, not_core, group)
        if group < 2:
            mine += turned(both, base_hi, base_lo, core, group)

    prod[...] = theirs[0:24] + theirs[24:48]
    give_r = pltpu.make_async_remote_copy(
        src_ref=prod, dst_ref=prod_got, send_sem=p_send, recv_sem=p_recv,
        device_id=partner, device_id_type=MESH,
    )
    give_r.start()
    mine += turned(both, base_hi, base_lo, core, 2)
    give_x.wait_send()

    @pl.when(core == 0)
    def _():
        for sub in range(6):
            hop0(RIGHT if sub < 3 else LEFT, sub).wait_send()

    @pl.when(core == 1)
    def _():
        for sub in range(6):
            hop0(LEFT, sub).wait_send()

    for way in range(2):
        for step in (1, 2, 3):
            for piece in range(5):
                hop(way, step, piece).wait_send()
    for group in range(3):
        each_over(group, lambda copy: copy.wait_send())
    give_r.wait()
    r_out[...] = mine[0:ROWS] + mine[24:24 + ROWS] + prod_got[0:ROWS, :]


def shards(tokens, factor_old, basis):
    tok_rows, features = tokens.shape
    scale_new = (1.0 - decay_rate) / (tok_rows * lax.axis_size("dp"))
    f32, bf16 = jnp.float32, jnp.bfloat16
    body = lambda *refs: kernel(scale_new, *refs)
    dma = pltpu.SemaphoreType.DMA
    return pl.pallas_call(
        body,
        name="gram_rotate",
        out_shape=(
            jax.ShapeDtypeStruct((ROWS, HALF), f32),
            jax.ShapeDtypeStruct((ROWS, HALF), f32),
        ),
        in_specs=[pl.BlockSpec(memory_space=pl.ANY)] * 3,
        out_specs=[pl.BlockSpec(memory_space=pltpu.VMEM)] * 2,
        scratch_shapes=[
            pltpu.VMEM((HALF, tok_rows), bf16),
            pltpu.VMEM((HALF, tok_rows), bf16),
            pltpu.VMEM((2 * HALF + 8, tok_rows), f32),
            pltpu.VMEM((192, tok_rows), f32),
            pltpu.VMEM((SIDE, LONG, 128), f32),
            pltpu.VMEM((LONG + 8, 128), f32),
            pltpu.VMEM((192, 128), f32),
            pltpu.VMEM((LONG, 128), bf16),
            pltpu.VMEM((LONG, 128), bf16),
            pltpu.VMEM((2, 3, LONG, 128), bf16),
            pltpu.VMEM((2, 3, LONG, 128), bf16),
            pltpu.VMEM((SIDE, 144, 128), f32),
            pltpu.VMEM((SIDE, 144, 128), bf16),
            pltpu.VMEM((SIDE - 1, 144, 128), bf16),
            pltpu.VMEM((ROWS, HALF), f32),
            pltpu.VMEM((HALF, 2 * HALF), f32),
            pltpu.VMEM((2, HALF, HALF), bf16),
            pltpu.VMEM((2, HALF, HALF), bf16),
            pltpu.VMEM((24, HALF), f32),
            pltpu.VMEM((24, HALF), f32),
            dma((3,)),
            dma((2,)),
            dma((6,)),
            dma((6,)),
            dma((2, 3, 5)),
            dma((2, 3, 5)),
            dma((SIDE - 1, 4)),
            dma((SIDE - 1, 4)),
            dma,
            dma,
            pltpu.SemaphoreType.REGULAR((3,)),
            pltpu.SemaphoreType.REGULAR,
            pltpu.SemaphoreType.REGULAR,
        ],
        compiler_params=pltpu.CompilerParams(
            collective_id=0, has_side_effects=True, vmem_limit_bytes=55040 * 1024
        ),
    )(tokens.T, factor_old, basis)


def solution(mesh):
    return jax.shard_map(
        shards,
        mesh=mesh,
        in_specs=(P("dp", "mp"), P("dp", "mp"), P("mp", None)),
        out_specs=(P("dp", "mp"), P("dp", "mp")),
        check_vma=False,
    )
```

```python
import jax
import jax.numpy as jnp
from jax import lax
from jax.experimental import pallas as pl
from jax.experimental.pallas import tpu as pltpu
from jax.sharding import PartitionSpec as P

decay_rate = 0.95

MESH = pl.DeviceIdType.MESH
SIDE = 8
ROWS = 21
CHUNK = SIDE * ROWS
HALF = 672
FULL = 5
REST = HALF - 128 * FULL
TILES = (0, CHUNK, 2 * CHUNK, 3 * CHUNK + 56, 4 * CHUNK + 56)
TAIL = 3 * CHUNK
LONG = 5 * CHUNK + 56
PIECES = ((0, 176), (176, 336), (336, 560), (560, 720), (720, LONG))
SUBS = ((0, 176), (176, 336), (336, 448), (448, 560), (560, 720), (720, LONG))
SUBS_OF = ((0,), (1,), (2, 3), (4,), (5,))
GROUPS = ((0, 1), (3, 4), (2,))
COLUMNS = ((0, 1), (3, 4), (2, 5))
RIGHT, LEFT = 0, 1
FAR = (4, 3, 5)
NEAR = (2, 6, 1, 7)
FIRST = (0, 1)


def encode(value):
    return ((value * jnp.abs(value)) * (value * value)).astype(jnp.bfloat16)


def decode(code):
    code = code.astype(jnp.float32)
    root = lax.rsqrt(lax.rsqrt(jnp.abs(code)))
    return jnp.where(code < 0.0, -root, root)


def spans(group):
    return [(128 * tile, min(128 * tile + 128, HALF)) for tile in COLUMNS[group]]


def turned(both, base_hi, base_lo, half, group):
    out = jnp.zeros((48, HALF), jnp.float32)
    for part, (lo, hi) in zip(both, spans(group)):
        out += jnp.dot(part, base_hi[half, lo:hi, :], preferred_element_type=jnp.float32)
        out += jnp.dot(part, base_lo[half, lo:hi, :], preferred_element_type=jnp.float32)
    return out


def kernel(
    scale_new, tok, old, bas, f_out, r_out,
    own_x, par_x, wide_x, left_x, gram, sums, rest, sent0, got0, sent, got, flat, codes, far, fac,
    base, base_hi, base_lo, prod, prod_got,
    load_sem, par_sem, z_send, z_recv, s_send, s_recv, t_send, t_recv,
    p_send, p_recv, ready, hello, go,
):
    dp, mp = lax.axis_index("dp"), lax.axis_index("mp")
    y, z, core = dp // SIDE, dp % SIDE, mp % 2
    not_core = 1 - core
    here = not_core * y + core * z
    across = core * y + not_core * z

    def along(step):
        to_y = (y + not_core * step + SIDE) % SIDE
        to_z = (z + core * step + SIDE) % SIDE
        return {"dp": to_y * SIDE + to_z, "mp": mp}

    def cross(step):
        to_y = (y + core * step + SIDE) % SIDE
        to_z = (z + not_core * step + SIDE) % SIDE
        return {"dp": to_y * SIDE + to_z, "mp": mp}

    partner = {"dp": dp, "mp": mp + 1 - 2 * core}

    load_x = pltpu.make_async_copy(tok, own_x, load_sem.at[0])
    load_b = pltpu.make_async_copy(bas, base, load_sem.at[1])
    load_f = pltpu.make_async_copy(old, fac, load_sem.at[2])
    load_x.start()
    barrier = pltpu.get_barrier_semaphore()
    for step in (1, -1):
        for to_y, to_z in (((y + step + SIDE) % SIDE, z), (y, (z + step + SIDE) % SIDE)):
            pl.semaphore_signal(
                barrier, inc=1, device_id={"dp": to_y * SIDE + to_z, "mp": mp - core},
                device_id_type=MESH,
            )
    give_x = pltpu.make_async_remote_copy(
        src_ref=tok, dst_ref=par_x, send_sem=par_sem.at[0], recv_sem=par_sem.at[1],
        device_id=partner, device_id_type=MESH,
    )

    @pl.when(core == 1)
    def _():
        pl.semaphore_wait(barrier, 1)
        pl.semaphore_signal(hello, inc=1, device_id=partner, device_id_type=MESH)
        give_x.start()

    @pl.when(core == 0)
    def _():
        pl.semaphore_signal(barrier, inc=1, device_id=partner, device_id_type=MESH)
        pl.semaphore_wait(hello, 1)
        give_x.start()

    load_b.start()
    load_f.start()
    wide_x[2 * HALF:2 * HALF + 8, :] = jnp.zeros((8, wide_x.shape[1]), jnp.float32)
    left_x[CHUNK:192, :] = jnp.zeros((192 - CHUNK, wide_x.shape[1]), jnp.float32)
    sums[LONG:LONG + 8, :] = jnp.zeros((8, 128), jnp.float32)
    for slot in range(SIDE):
        gram[slot, TAIL + 48:TAIL + 56, :] = jnp.zeros((8, 128), jnp.float32)

    def announce(number):
        for device in (cross(1), cross(-1)):
            pl.semaphore_signal(
                ready.at[number], inc=1, device_id=device, device_id_type=MESH
            )

    load_x.wait()
    wide_x[pl.ds(pl.multiple_of(HALF * core, 8), HALF), :] = own_x[...].astype(jnp.float32)
    alone = (core == 0) & (y >= SIDE // 2)

    def take_x():
        give_x.wait_recv()
        wide_x[pl.ds(pl.multiple_of(HALF * not_core, 8), HALF), :] = par_x[...].astype(jnp.float32)

    pl.when(jnp.logical_not(alone))(take_x)

    def products(slot, position):
        for group in range(SIDE):
            in_y = CHUNK * position + ROWS * group
            in_z = ROWS * position + CHUNK * group
            start = not_core * in_y + core * in_z
            block = wide_x[pl.ds(pl.multiple_of(start // 8 * 8, 8), 32), :]
            block = pltpu.roll(block, (32 - start % 8) % 32, 0)
            left_x[ROWS * group:ROWS * group + 24, :] = block[0:24]
        left = left_x[...].astype(jnp.bfloat16)
        main = lax.dot_general(
            left[0:176], own_x[0:128 * FULL, :], (((1,), (1,)), ((), ())),
            preferred_element_type=jnp.float32,
        )
        for tile in range(FULL):
            gram[slot, TILES[tile]:TILES[tile] + CHUNK, :] = main[0:CHUNK, 128 * tile:128 * (tile + 1)]
        thin = lax.dot_general(
            left, own_x[128 * FULL:HALF, :], (((1,), (1,)), ((), ())),
            preferred_element_type=jnp.float32,
        )
        gram[slot, TAIL:TAIL + 48, :] = jnp.concatenate(
            [thin[48 * k:48 * (k + 1)] for k in range(4)], 1
        )

    def slot_of(way, step):
        return 0 if step == 0 else 2 * step - 1 + way

    def hop0(way, sub):
        lo, hi = SUBS[sub]
        return pltpu.make_async_remote_copy(
            src_ref=sent0.at[pl.ds(lo, hi - lo)], dst_ref=got0.at[pl.ds(lo, hi - lo)],
            send_sem=z_send.at[sub], recv_sem=z_recv.at[sub],
            device_id=along(1 if way == RIGHT else -1), device_id_type=MESH,
        )

    def hop(way, step, piece):
        lo, hi = PIECES[piece]
        return pltpu.make_async_remote_copy(
            src_ref=sent.at[way, step - 1, pl.ds(lo, hi - lo)],
            dst_ref=got.at[way, step - 1, pl.ds(lo, hi - lo)],
            send_sem=s_send.at[way, step - 1, piece], recv_sem=s_recv.at[way, step - 1, piece],
            device_id=along(1 if way == RIGHT else -1), device_id_type=MESH,
        )

    def put(way, step, piece, first=()):
        slot = slot_of(way, step)
        lo, hi = PIECES[piece]
        if step == 1:
            for sub in SUBS_OF[piece]:
                a, b = SUBS[sub]
                total = gram[slot, a:b, :]
                if sub in first:
                    hop0(way, sub).wait_recv()
                    total = total + decode(got0[a:b, :])
                sent[way, 0, a:b, :] = encode(total)
        else:
            hop(way, step - 1, piece).wait_recv()
            sent[way, step - 1, lo:hi, :] = encode(
                gram[slot, lo:hi, :] + decode(got[way, step - 2, lo:hi, :])
            )
        hop(way, step, piece).start()

    def split_base(first, last):
        @pl.loop(first, last)
        def _(part):
            at = pl.ds(pl.multiple_of(part * 96, 96), 96)
            for half in range(2):
                value = base[at, HALF * half:HALF * (half + 1)]
                high = value.astype(jnp.bfloat16)
                base_hi[half, at, :] = high
                base_lo[half, at, :] = (value - high.astype(jnp.float32)).astype(jnp.bfloat16)

    every = (0, 1, 3, 4, 2)
    ahead = ((3, 4, 0, 1, 2), (1, 0, 4, 3, 2))

    def first_chunk():
        products(0, (here + 4) % SIDE)
        sent0[...] = encode(gram[0])

    @pl.when(core == 0)
    def _():
        first_chunk()
        pl.semaphore_wait(barrier, 8)
        pl.semaphore_signal(go, inc=1, device_id=partner, device_id_type=MESH)
        for right, left in ((0, 5), (1, 4), (2, 3)):
            hop0(RIGHT, right).start()
            hop0(LEFT, left).start()

    @pl.when(core == 1)
    def _():
        products(1, (here + 3) % SIDE)
        pl.semaphore_wait(go, 1)
        for piece in every:
            put(RIGHT, 1, piece)
        first_chunk()
        for sub in (0, 1, 4, 5, 2, 3):
            hop0(LEFT, sub).start()

    pl.when(alone)(take_x)
    announce(0)

    def chunk(slot):
        products(slot, (here + (0, 3, 5, 2, 6, 1, 7, 0)[slot]) % SIDE)

    @pl.when(core == 0)
    def _():
        chunk(1)
        for place in (0, 1):
            put(RIGHT, 1, ahead[RIGHT][place])
        chunk(2)
        for place in (0, 1):
            put(LEFT, 1, ahead[LEFT][place])
        chunk(3)
        chunk(4)
        for place in (2, 3, 4):
            put(RIGHT, 1, ahead[RIGHT][place], (0, 1, 2))
            put(LEFT, 1, ahead[LEFT][place], (3, 4, 5))

    @pl.when(core == 1)
    def _():
        chunk(2)
        chunk(3)
        for piece in every:
            put(RIGHT, 2, piece)
            put(LEFT, 1, piece, range(6))

    pl.semaphore_wait(ready.at[0], 2)
    announce(1)

    @pl.when(core == 0)
    def _():
        for place in range(5):
            put(RIGHT, 2, ahead[RIGHT][place])
            put(LEFT, 2, ahead[LEFT][place])
        chunk(5)
        chunk(6)

    @pl.when(core == 1)
    def _():
        chunk(5)
        chunk(4)
        for piece in every:
            put(RIGHT, 3, piece)
            put(LEFT, 2, piece)
        chunk(6)

    pl.semaphore_wait(ready.at[1], 2)
    announce(2)

    @pl.when(core == 0)
    def _():
        for place in range(5):
            put(RIGHT, 3, ahead[RIGHT][place])
            put(LEFT, 3, ahead[LEFT][place])

    @pl.when(core == 1)
    def _():
        for piece in every:
            put(LEFT, 3, piece)

    chunk(7)
    pl.semaphore_wait(ready.at[2], 2)

    PAIR = 3

    def over(to, group):
        away = (to - across + SIDE) % SIDE
        slot = away - 1
        at = pl.ds(0, 96) if group == PAIR else pl.ds(48 * group, 48)
        return pltpu.make_async_remote_copy(
            src_ref=codes.at[to, at], dst_ref=far.at[slot, at],
            send_sem=t_send.at[slot, group], recv_sem=t_recv.at[slot, group],
            device_id=cross(away), device_id_type=MESH,
        )

    def each_over(group, act):
        def send(to, single):
            if single or group == 2:
                act(over(to, group))
            elif group == 1:
                act(over(to, PAIR))

        @pl.when(core == 0)
        def _():
            for to in range(SIDE):
                @pl.when(across != to)
                def _():
                    send(to, to in FIRST)

        @pl.when(core == 1)
        def _():
            for step in FAR:
                send((across + step) % SIDE, True)
            for step in NEAR:
                send((across + step) % SIDE, False)

    def landed(group):
        def one(step, single):
            if single or group == 2:
                over((across + step) % SIDE, group).wait_recv()
            elif group == 0:
                over((across + step) % SIDE, PAIR).wait_recv()

        @pl.when(core == 1)
        def _():
            for step in FAR:
                one(step, True)
            for step in NEAR:
                one(step, False)

        @pl.when((core == 0) & (across < len(FIRST)))
        def _():
            for step in range(1, SIDE):
                one(step, True)

        @pl.when((core == 0) & (across >= len(FIRST)))
        def _():
            for step in range(1, SIDE):
                one(step, False)

    for group, pieces in enumerate(GROUPS):
        for piece in pieces:
            lo, hi = PIECES[piece]
            hop(RIGHT, 3, piece).wait_recv()
            hop(LEFT, 3, piece).wait_recv()
            sums[lo:hi, :] = (
                gram[7, lo:hi, :] + decode(got[RIGHT, 2, lo:hi, :]) + decode(got[LEFT, 2, lo:hi, :])
            )
        if 2 in pieces:
            for k in range(4):
                rest[48 * k:48 * (k + 1), 0:REST] = sums[TAIL:TAIL + 48, REST * k:REST * (k + 1)]
        for to in range(SIDE):
            parts = []
            for tile in COLUMNS[group]:
                if tile < FULL:
                    at = TILES[tile] + ROWS * to
                    parts.append(sums[at:at + 24, :])
                else:
                    parts.append(rest[ROWS * to:ROWS * to + 24, :])
            both = jnp.concatenate(parts, 0)
            flat[to, 48 * group:48 * group + 48, :] = both
            codes[to, 48 * group:48 * group + 48, :] = encode(both)
        each_over(group, lambda copy: copy.start())

    load_b.wait()
    split_base(0, 7)
    load_f.wait()
    theirs = jnp.zeros((48, HALF), jnp.float32)
    mine = jnp.zeros((48, HALF), jnp.float32)
    for group in range(3):
        total = flat[across, 48 * group:48 * group + 48, :]
        landed(group)
        for slot in range(SIDE - 1):
            total += decode(far[slot, 48 * group:48 * group + 48, :])
        both = []
        for k, (lo, hi) in enumerate(spans(group)):
            new = decay_rate * fac[:, lo:hi] + scale_new * total[24 * k:24 * k + ROWS, 0:hi - lo]
            f_out[:, lo:hi] = new
            new = jnp.concatenate([new, jnp.zeros((24 - ROWS, hi - lo), jnp.float32)], 0)
            high = new.astype(jnp.bfloat16).astype(jnp.float32)
            both.append(jnp.concatenate([high, new - high], 0).astype(jnp.bfloat16))
        theirs += turned(both, base_hi, base_lo, not_core, group)
        if group < 2:
            mine += turned(both, base_hi, base_lo, core, group)

    prod[...] = theirs[0:24] + theirs[24:48]
    give_r = pltpu.make_async_remote_copy(
        src_ref=prod, dst_ref=prod_got, send_sem=p_send, recv_sem=p_recv,
        device_id=partner, device_id_type=MESH,
    )
    give_r.start()
    mine += turned(both, base_hi, base_lo, core, 2)
    give_x.wait_send()

    @pl.when(core == 0)
    def _():
        for sub in range(6):
            hop0(RIGHT if sub < 3 else LEFT, sub).wait_send()

    @pl.when(core == 1)
    def _():
        for sub in range(6):
            hop0(LEFT, sub).wait_send()

    for way in range(2):
        for step in (1, 2, 3):
            for piece in range(5):
                hop(way, step, piece).wait_send()
    for group in range(3):
        each_over(group, lambda copy: copy.wait_send())
    give_r.wait()
    r_out[...] = mine[0:ROWS] + mine[24:24 + ROWS] + prod_got[0:ROWS, :]


def shards(tokens, factor_old, basis):
    tok_rows, features = tokens.shape
    scale_new = (1.0 - decay_rate) / (tok_rows * lax.axis_size("dp"))
    f32, bf16 = jnp.float32, jnp.bfloat16
    body = lambda *refs: kernel(scale_new, *refs)
    dma = pltpu.SemaphoreType.DMA
    factor, rotated = pl.pallas_call(
        body,
        name="gram_rotate",
        out_shape=(
            jax.ShapeDtypeStruct((ROWS, HALF), f32),
            jax.ShapeDtypeStruct((ROWS, HALF), f32),
        ),
        in_specs=[pl.BlockSpec(memory_space=pl.ANY)] * 3,
        out_specs=[pl.BlockSpec(memory_space=pltpu.VMEM)] * 2,
        scratch_shapes=[
            pltpu.VMEM((HALF, tok_rows), bf16),
            pltpu.VMEM((HALF, tok_rows), bf16),
            pltpu.VMEM((2 * HALF + 8, tok_rows), f32),
            pltpu.VMEM((192, tok_rows), f32),
            pltpu.VMEM((SIDE, LONG, 128), f32),
            pltpu.VMEM((LONG + 8, 128), f32),
            pltpu.VMEM((192, 128), f32),
            pltpu.VMEM((LONG, 128), bf16),
            pltpu.VMEM((LONG, 128), bf16),
            pltpu.VMEM((2, 3, LONG, 128), bf16),
            pltpu.VMEM((2, 3, LONG, 128), bf16),
            pltpu.VMEM((SIDE, 144, 128), f32),
            pltpu.VMEM((SIDE, 144, 128), bf16),
            pltpu.VMEM((SIDE - 1, 144, 128), bf16),
            pltpu.VMEM((ROWS, HALF), f32),
            pltpu.VMEM((HALF, 2 * HALF), f32),
            pltpu.VMEM((2, HALF, HALF), bf16),
            pltpu.VMEM((2, HALF, HALF), bf16),
            pltpu.VMEM((24, HALF), f32),
            pltpu.VMEM((24, HALF), f32),
            dma((3,)),
            dma((2,)),
            dma((6,)),
            dma((6,)),
            dma((2, 3, 5)),
            dma((2, 3, 5)),
            dma((SIDE - 1, 4)),
            dma((SIDE - 1, 4)),
            dma,
            dma,
            pltpu.SemaphoreType.REGULAR((3,)),
            pltpu.SemaphoreType.REGULAR,
            pltpu.SemaphoreType.REGULAR,
        ],
        compiler_params=pltpu.CompilerParams(
            collective_id=0, has_side_effects=True, vmem_limit_bytes=55040 * 1024
        ),
    )(tokens.T, factor_old, basis)
    return factor + 0.0 * rotated, rotated + 0.0 * factor


def solution(mesh):
    return jax.shard_map(
        shards,
        mesh=mesh,
        in_specs=(P("dp", "mp"), P("dp", "mp"), P("mp", None)),
        out_specs=(P("dp", "mp"), P("dp", "mp")),
        check_vma=False,
    )
```

```python
import jax
import jax.numpy as jnp
from jax import lax
from jax.experimental import pallas as pl
from jax.experimental.pallas import tpu as pltpu
from jax.sharding import PartitionSpec as P

decay_rate = 0.95

MESH = pl.DeviceIdType.MESH
SIDE = 8
ROWS = 21
CHUNK = SIDE * ROWS
HALF = 672
FULL = 5
REST = HALF - 128 * FULL
TILES = (0, CHUNK, 2 * CHUNK, 3 * CHUNK + 56, 4 * CHUNK + 56)
TAIL = 3 * CHUNK
LONG = 5 * CHUNK + 56
PIECES = ((0, 176), (176, 336), (336, 560), (560, 720), (720, LONG))
SUBS = ((0, 176), (176, 336), (336, 448), (448, 560), (560, 720), (720, LONG))
SUBS_OF = ((0,), (1,), (2, 3), (4,), (5,))
GROUPS = ((0, 1), (3, 4), (2,))
COLUMNS = ((0, 1), (3, 4), (2, 5))
RIGHT, LEFT = 0, 1
FAR = (4, 3, 5)
NEAR = (2, 6, 1, 7)
FIRST = (0, 1)


def encode(value):
    return ((value * jnp.abs(value)) * (value * value)).astype(jnp.bfloat16)


def decode(code):
    code = code.astype(jnp.float32)
    root = lax.rsqrt(lax.rsqrt(jnp.abs(code)))
    return jnp.where(code < 0.0, -root, root)


def spans(group):
    return [(128 * tile, min(128 * tile + 128, HALF)) for tile in COLUMNS[group]]


def turned(both, base_hi, base_lo, half, group):
    out = jnp.zeros((48, HALF), jnp.float32)
    for part, (lo, hi) in zip(both, spans(group)):
        out += jnp.dot(part, base_hi[half, lo:hi, :], preferred_element_type=jnp.float32)
        out += jnp.dot(part, base_lo[half, lo:hi, :], preferred_element_type=jnp.float32)
    return out


def kernel(
    scale_new, tok, old, bas, f_out, r_out,
    own_x, par_x, wide_x, left_x, gram, sums, rest, sent0, got0, sent, got, flat, codes, far, fac,
    base, base_hi, base_lo, prod, prod_got,
    load_sem, par_sem, z_send, z_recv, s_send, s_recv, t_send, t_recv,
    p_send, p_recv, ready, hello, go,
):
    dp, mp = lax.axis_index("dp"), lax.axis_index("mp")
    y, z, core = dp // SIDE, dp % SIDE, mp % 2
    not_core = 1 - core
    here = not_core * y + core * z
    across = core * y + not_core * z

    def along(step):
        to_y = (y + not_core * step + SIDE) % SIDE
        to_z = (z + core * step + SIDE) % SIDE
        return {"dp": to_y * SIDE + to_z, "mp": mp}

    def cross(step):
        to_y = (y + core * step + SIDE) % SIDE
        to_z = (z + not_core * step + SIDE) % SIDE
        return {"dp": to_y * SIDE + to_z, "mp": mp}

    partner = {"dp": dp, "mp": mp + 1 - 2 * core}

    load_x = pltpu.make_async_copy(tok, own_x, load_sem.at[0])
    load_b = pltpu.make_async_copy(bas, base, load_sem.at[1])
    load_f = pltpu.make_async_copy(old, fac, load_sem.at[2])
    load_x.start()
    barrier = pltpu.get_barrier_semaphore()
    for step in (1, -1):
        for to_y, to_z in (((y + step + SIDE) % SIDE, z), (y, (z + step + SIDE) % SIDE)):
            pl.semaphore_signal(
                barrier, inc=1, device_id={"dp": to_y * SIDE + to_z, "mp": mp - core},
                device_id_type=MESH,
            )
    give_x = pltpu.make_async_remote_copy(
        src_ref=tok, dst_ref=par_x, send_sem=par_sem.at[0], recv_sem=par_sem.at[1],
        device_id=partner, device_id_type=MESH,
    )

    @pl.when(core == 1)
    def _():
        pl.semaphore_wait(barrier, 1)
        pl.semaphore_signal(hello, inc=1, device_id=partner, device_id_type=MESH)
        give_x.start()

    @pl.when(core == 0)
    def _():
        pl.semaphore_signal(barrier, inc=1, device_id=partner, device_id_type=MESH)
        pl.semaphore_wait(hello, 1)
        give_x.start()

    load_b.start()
    load_f.start()
    wide_x[2 * HALF:2 * HALF + 8, :] = jnp.zeros((8, wide_x.shape[1]), jnp.float32)
    left_x[CHUNK:192, :] = jnp.zeros((192 - CHUNK, wide_x.shape[1]), jnp.float32)
    sums[LONG:LONG + 8, :] = jnp.zeros((8, 128), jnp.float32)
    for slot in range(SIDE):
        gram[slot, TAIL + 48:TAIL + 56, :] = jnp.zeros((8, 128), jnp.float32)

    def announce(number):
        for device in (cross(1), cross(-1)):
            pl.semaphore_signal(
                ready.at[number], inc=1, device_id=device, device_id_type=MESH
            )

    load_x.wait()
    wide_x[pl.ds(pl.multiple_of(HALF * core, 8), HALF), :] = own_x[...].astype(jnp.float32)
    alone = (core == 0) & (y >= SIDE // 2)

    def take_x():
        give_x.wait_recv()
        wide_x[pl.ds(pl.multiple_of(HALF * not_core, 8), HALF), :] = par_x[...].astype(jnp.float32)

    pl.when(jnp.logical_not(alone))(take_x)

    def products(slot, position):
        for group in range(SIDE):
            in_y = CHUNK * position + ROWS * group
            in_z = ROWS * position + CHUNK * group
            start = not_core * in_y + core * in_z
            block = wide_x[pl.ds(pl.multiple_of(start // 8 * 8, 8), 32), :]
            block = pltpu.roll(block, (32 - start % 8) % 32, 0)
            left_x[ROWS * group:ROWS * group + 24, :] = block[0:24]
        left = left_x[...].astype(jnp.bfloat16)
        main = lax.dot_general(
            left[0:176], own_x[0:128 * FULL, :], (((1,), (1,)), ((), ())),
            preferred_element_type=jnp.float32,
        )
        for tile in range(FULL):
            gram[slot, TILES[tile]:TILES[tile] + CHUNK, :] = main[0:CHUNK, 128 * tile:128 * (tile + 1)]
        thin = lax.dot_general(
            left, own_x[128 * FULL:HALF, :], (((1,), (1,)), ((), ())),
            preferred_element_type=jnp.float32,
        )
        gram[slot, TAIL:TAIL + 48, :] = jnp.concatenate(
            [thin[48 * k:48 * (k + 1)] for k in range(4)], 1
        )

    def slot_of(way, step):
        return 0 if step == 0 else 2 * step - 1 + way

    def hop0(way, sub):
        lo, hi = SUBS[sub]
        return pltpu.make_async_remote_copy(
            src_ref=sent0.at[pl.ds(lo, hi - lo)], dst_ref=got0.at[pl.ds(lo, hi - lo)],
            send_sem=z_send.at[sub], recv_sem=z_recv.at[sub],
            device_id=along(1 if way == RIGHT else -1), device_id_type=MESH,
        )

    def hop(way, step, piece):
        lo, hi = PIECES[piece]
        return pltpu.make_async_remote_copy(
            src_ref=sent.at[way, step - 1, pl.ds(lo, hi - lo)],
            dst_ref=got.at[way, step - 1, pl.ds(lo, hi - lo)],
            send_sem=s_send.at[way, step - 1, piece], recv_sem=s_recv.at[way, step - 1, piece],
            device_id=along(1 if way == RIGHT else -1), device_id_type=MESH,
        )

    def put(way, step, piece, first=()):
        slot = slot_of(way, step)
        lo, hi = PIECES[piece]
        if step == 1:
            for sub in SUBS_OF[piece]:
                a, b = SUBS[sub]
                total = gram[slot, a:b, :]
                if sub in first:
                    hop0(way, sub).wait_recv()
                    total = total + decode(got0[a:b, :])
                sent[way, 0, a:b, :] = encode(total)
        else:
            hop(way, step - 1, piece).wait_recv()
            sent[way, step - 1, lo:hi, :] = encode(
                gram[slot, lo:hi, :] + decode(got[way, step - 2, lo:hi, :])
            )
        hop(way, step, piece).start()

    def split_base(first, last):
        @pl.loop(first, last)
        def _(part):
            at = pl.ds(pl.multiple_of(part * 96, 96), 96)
            for half in range(2):
                value = base[at, HALF * half:HALF * (half + 1)]
                high = value.astype(jnp.bfloat16)
                base_hi[half, at, :] = high
                base_lo[half, at, :] = (value - high.astype(jnp.float32)).astype(jnp.bfloat16)

    every = (0, 1, 3, 4, 2)
    ahead = ((3, 4, 0, 1, 2), (1, 0, 4, 3, 2))

    def first_chunk():
        products(0, (here + 4) % SIDE)
        sent0[...] = encode(gram[0])

    @pl.when(core == 0)
    def _():
        first_chunk()
        pl.semaphore_wait(barrier, 8)
        pl.semaphore_signal(go, inc=1, device_id=partner, device_id_type=MESH)
        for right, left in ((0, 5), (1, 4), (2, 3)):
            hop0(RIGHT, right).start()
            hop0(LEFT, left).start()

    @pl.when(core == 1)
    def _():
        products(1, (here + 3) % SIDE)
        pl.semaphore_wait(go, 1)
        for piece in every:
            put(RIGHT, 1, piece)
        first_chunk()
        for sub in (0, 1, 4, 5, 2, 3):
            hop0(LEFT, sub).start()

    pl.when(alone)(take_x)
    announce(0)

    def chunk(slot):
        products(slot, (here + (0, 3, 5, 2, 6, 1, 7, 0)[slot]) % SIDE)

    @pl.when(core == 0)
    def _():
        chunk(1)
        for place in (0, 1):
            put(RIGHT, 1, ahead[RIGHT][place])
        chunk(2)
        for place in (0, 1):
            put(LEFT, 1, ahead[LEFT][place])
        chunk(3)
        chunk(4)
        for place in (2, 3, 4):
            put(RIGHT, 1, ahead[RIGHT][place], (0, 1, 2))
            put(LEFT, 1, ahead[LEFT][place], (3, 4, 5))

    @pl.when(core == 1)
    def _():
        chunk(2)
        chunk(3)
        for piece in every:
            put(RIGHT, 2, piece)
            put(LEFT, 1, piece, range(6))

    pl.semaphore_wait(ready.at[0], 2)
    announce(1)

    @pl.when(core == 0)
    def _():
        for place in range(5):
            put(RIGHT, 2, ahead[RIGHT][place])
            put(LEFT, 2, ahead[LEFT][place])
        chunk(5)
        chunk(6)

    @pl.when(core == 1)
    def _():
        chunk(5)
        chunk(4)
        for piece in every:
            put(RIGHT, 3, piece)
            put(LEFT, 2, piece)
        chunk(6)

    pl.semaphore_wait(ready.at[1], 2)
    announce(2)

    @pl.when(core == 0)
    def _():
        for place in range(5):
            put(RIGHT, 3, ahead[RIGHT][place])
            put(LEFT, 3, ahead[LEFT][place])

    @pl.when(core == 1)
    def _():
        for piece in every:
            put(LEFT, 3, piece)

    chunk(7)
    pl.semaphore_wait(ready.at[2], 2)

    PAIR = 3

    def over(to, group):
        away = (to - across + SIDE) % SIDE
        slot = away - 1
        at = pl.ds(0, 96) if group == PAIR else pl.ds(48 * group, 48)
        return pltpu.make_async_remote_copy(
            src_ref=codes.at[to, at], dst_ref=far.at[slot, at],
            send_sem=t_send.at[slot, group], recv_sem=t_recv.at[slot, group],
            device_id=cross(away), device_id_type=MESH,
        )

    def each_over(group, act):
        def send(to, single):
            if single or group == 2:
                act(over(to, group))
            elif group == 1:
                act(over(to, PAIR))

        @pl.when(core == 0)
        def _():
            for to in range(SIDE):
                @pl.when(across != to)
                def _():
                    send(to, to in FIRST)

        @pl.when(core == 1)
        def _():
            for step in FAR:
                send((across + step) % SIDE, True)
            for step in NEAR:
                send((across + step) % SIDE, False)

    def landed(group):
        def one(step, single):
            if single or group == 2:
                over((across + step) % SIDE, group).wait_recv()
            elif group == 0:
                over((across + step) % SIDE, PAIR).wait_recv()

        @pl.when(core == 1)
        def _():
            for step in FAR:
                one(step, True)
            for step in NEAR:
                one(step, False)

        @pl.when((core == 0) & (across < len(FIRST)))
        def _():
            for step in range(1, SIDE):
                one(step, True)

        @pl.when((core == 0) & (across >= len(FIRST)))
        def _():
            for step in range(1, SIDE):
                one(step, False)

    for group, pieces in enumerate(GROUPS):
        for piece in pieces:
            lo, hi = PIECES[piece]
            hop(RIGHT, 3, piece).wait_recv()
            hop(LEFT, 3, piece).wait_recv()
            sums[lo:hi, :] = (
                gram[7, lo:hi, :] + decode(got[RIGHT, 2, lo:hi, :]) + decode(got[LEFT, 2, lo:hi, :])
            )
        if 2 in pieces:
            for k in range(4):
                rest[48 * k:48 * (k + 1), 0:REST] = sums[TAIL:TAIL + 48, REST * k:REST * (k + 1)]
        for to in range(SIDE):
            parts = []
            for tile in COLUMNS[group]:
                if tile < FULL:
                    at = TILES[tile] + ROWS * to
                    parts.append(sums[at:at + 24, :])
                else:
                    parts.append(rest[ROWS * to:ROWS * to + 24, :])
            both = jnp.concatenate(parts, 0)
            flat[to, 48 * group:48 * group + 48, :] = both
            codes[to, 48 * group:48 * group + 48, :] = encode(both)
        each_over(group, lambda copy: copy.start())

    load_b.wait()
    split_base(0, 7)
    give_x.wait_send()

    @pl.when(core == 0)
    def _():
        for sub in range(6):
            hop0(RIGHT if sub < 3 else LEFT, sub).wait_send()

    @pl.when(core == 1)
    def _():
        for sub in range(6):
            hop0(LEFT, sub).wait_send()

    for way in range(2):
        for step in (1, 2, 3):
            for piece in range(5):
                hop(way, step, piece).wait_send()
    load_f.wait()
    theirs = jnp.zeros((48, HALF), jnp.float32)
    mine = jnp.zeros((48, HALF), jnp.float32)
    for group in range(3):
        total = flat[across, 48 * group:48 * group + 48, :]
        landed(group)
        for slot in range(SIDE - 1):
            total += decode(far[slot, 48 * group:48 * group + 48, :])
        both = []
        for k, (lo, hi) in enumerate(spans(group)):
            new = decay_rate * fac[:, lo:hi] + scale_new * total[24 * k:24 * k + ROWS, 0:hi - lo]
            f_out[:, lo:hi] = new
            new = jnp.concatenate([new, jnp.zeros((24 - ROWS, hi - lo), jnp.float32)], 0)
            high = new.astype(jnp.bfloat16).astype(jnp.float32)
            both.append(jnp.concatenate([high, new - high], 0).astype(jnp.bfloat16))
        theirs += turned(both, base_hi, base_lo, not_core, group)
        if group < 2:
            mine += turned(both, base_hi, base_lo, core, group)

    prod[...] = theirs[0:24] + theirs[24:48]
    give_r = pltpu.make_async_remote_copy(
        src_ref=prod, dst_ref=prod_got, send_sem=p_send, recv_sem=p_recv,
        device_id=partner, device_id_type=MESH,
    )
    give_r.start()
    mine += turned(both, base_hi, base_lo, core, 2)
    for group in range(3):
        each_over(group, lambda copy: copy.wait_send())
    give_r.wait()
    r_out[...] = mine[0:ROWS] + mine[24:24 + ROWS] + prod_got[0:ROWS, :]


def shards(tokens, factor_old, basis):
    tok_rows, features = tokens.shape
    scale_new = (1.0 - decay_rate) / (tok_rows * lax.axis_size("dp"))
    f32, bf16 = jnp.float32, jnp.bfloat16
    body = lambda *refs: kernel(scale_new, *refs)
    dma = pltpu.SemaphoreType.DMA
    factor, rotated = pl.pallas_call(
        body,
        name="gram_rotate",
        out_shape=(
            jax.ShapeDtypeStruct((ROWS, HALF), f32),
            jax.ShapeDtypeStruct((ROWS, HALF), f32),
        ),
        in_specs=[pl.BlockSpec(memory_space=pl.ANY)] * 3,
        out_specs=[pl.BlockSpec(memory_space=pltpu.VMEM)] * 2,
        scratch_shapes=[
            pltpu.VMEM((HALF, tok_rows), bf16),
            pltpu.VMEM((HALF, tok_rows), bf16),
            pltpu.VMEM((2 * HALF + 8, tok_rows), f32),
            pltpu.VMEM((192, tok_rows), f32),
            pltpu.VMEM((SIDE, LONG, 128), f32),
            pltpu.VMEM((LONG + 8, 128), f32),
            pltpu.VMEM((192, 128), f32),
            pltpu.VMEM((LONG, 128), bf16),
            pltpu.VMEM((LONG, 128), bf16),
            pltpu.VMEM((2, 3, LONG, 128), bf16),
            pltpu.VMEM((2, 3, LONG, 128), bf16),
            pltpu.VMEM((SIDE, 144, 128), f32),
            pltpu.VMEM((SIDE, 144, 128), bf16),
            pltpu.VMEM((SIDE - 1, 144, 128), bf16),
            pltpu.VMEM((ROWS, HALF), f32),
            pltpu.VMEM((HALF, 2 * HALF), f32),
            pltpu.VMEM((2, HALF, HALF), bf16),
            pltpu.VMEM((2, HALF, HALF), bf16),
            pltpu.VMEM((24, HALF), f32),
            pltpu.VMEM((24, HALF), f32),
            dma((3,)),
            dma((2,)),
            dma((6,)),
            dma((6,)),
            dma((2, 3, 5)),
            dma((2, 3, 5)),
            dma((SIDE - 1, 4)),
            dma((SIDE - 1, 4)),
            dma,
            dma,
            pltpu.SemaphoreType.REGULAR((3,)),
            pltpu.SemaphoreType.REGULAR,
            pltpu.SemaphoreType.REGULAR,
        ],
        compiler_params=pltpu.CompilerParams(
            collective_id=0, has_side_effects=True, vmem_limit_bytes=55040 * 1024
        ),
    )(tokens.T, factor_old, basis)
    return factor + 0.0 * rotated, rotated + 0.0 * factor


def solution(mesh):
    return jax.shard_map(
        shards,
        mesh=mesh,
        in_specs=(P("dp", "mp"), P("dp", "mp"), P("mp", None)),
        out_specs=(P("dp", "mp"), P("dp", "mp")),
        check_vma=False,
    )
```
